256 devices in a mesh: sub: 8 (over x, core), grp: 32 (over z, y).
Axes of the slice: x: 4, y: 4, z: 8, core: 2. Of those that a mesh axis runs over, the one named last changes fastest.
Arguments:
- rhs: float32 [32, 8, 2048, 128], P('grp', 'sub')
- schur: bfloat16 [32, 8, 2048, 2048], P('grp', 'sub'), as said below
- stiff: float32 [32, 8, 2048], P('grp', 'sub'), may hold values from 1 to 100
- face_index: int32 [32, 8, 2048], P('grp', 'sub'), may hold values from 0 to 2047, each once within a row
- basis: bfloat16 [32, 8, 2048, 256], P('grp', 'sub'), may hold values from -0.125 to 0.125
- membership: int32 [32, 256], P('grp'), may hold values from 0 to 255
- level1_inv: float32 [32, 256, 256], P('grp'), as said below
- level2_inv: float32 [256, 256], replicated, as said below
Outputs:
- solution: float32 [32, 8, 2048, 128], P('grp', 'sub')
- residual: float32 [32, 8, 2048, 128], P('grp', 'sub')
The draws below stay inside these ranges and needn't reach their ends.
Inputs may be any that keep to these rules, and one draw needn't show every extreme that they name: `face_index`: each subdomain's row is a permutation of 0 to 2047; the matching of blocks between neighbours is as in the reference program. `schur`: each subdomain's matrix is symmetric positive definite. `level1_inv`: each group's matrix is symmetric positive definite. `level2_inv`: symmetric positive definite.
All inputs are finite; a program needn't handle non-finite values.
Results may differ from the reference program's by a relative error of at most 0.015.
Values sent between devices are 32-bit elements; how exact they have to be, the bound alone decides.
No kernel may reach another device: no remote copies, remote signals or barrier semaphores. Data moves between devices by JAX's collectives and lax.ppermute only.
A program may use at most 64 MiB of HBM per device.

```python
import math
import jax
import jax.numpy as jnp
from jax import lax

NI = 2048
RHS = 128
G1 = 256
G2 = 256
ITERS = 2
LOCAL_STEPS = 2
N_SUB = 8
N_GRP = 32


def dominant(key, leading, size_n, low, high, spread):
    key_a, key_b = jax.random.split(key)
    raw = jax.random.uniform(key_a, leading + (size_n, size_n), jnp.float32, -1.0, 1.0)
    symmetric = (raw + jnp.swapaxes(raw, -1, -2)) * (spread * math.sqrt(1.5) / math.sqrt(size_n))
    spot = jax.random.uniform(key_b, leading + (size_n,), jnp.float32, 0.0, 1.0)
    diag_vals = low * jnp.exp(spot * math.log(high / low))
    identity = jnp.eye(size_n, dtype=jnp.float32)
    return symmetric * (1.0 - identity) + identity * diag_vals[..., None]


def draw_schur(key, part):
    key = jax.random.fold_in(key, 3)
    return dominant(key, (N_GRP, N_SUB), NI, 1.0, 3.0, 0.3).astype(jnp.bfloat16)


def draw_level1_inv(key, part):
    key = jax.random.fold_in(key, 5)
    return dominant(key, (N_GRP,), G1, 0.5, 1.5, 0.3)


def draw_level2_inv(key, part):
    key = jax.random.fold_in(key, 7)
    return dominant(key, (), G2, 0.5, 1.5, 0.3)


def draw_rhs(key, part):
    key = jax.random.fold_in(key, 11)
    key_a, key_b = jax.random.split(key)
    shape_all = (N_GRP, N_SUB, NI, RHS)
    position = (jnp.arange(N_GRP)[:, None] * N_SUB + jnp.arange(N_SUB)[None, :]).astype(jnp.float32)
    ramp = jnp.exp(position / max(N_GRP * N_SUB - 1, 1) * math.log(3.0))
    row_scale = jnp.exp(jax.random.uniform(key_b, (N_GRP, N_SUB, NI, 1), jnp.float32, 0.0, math.log(10.0)))
    base = jax.random.normal(key_a, shape_all, jnp.float32)
    return base * row_scale * ramp[:, :, None, None]


def plant(drawn, key, smallest, high):
    spot = [jax.random.randint(jax.random.fold_in(key, axis), (), 0, length) for axis, length in enumerate(drawn.shape)]
    widest = drawn.shape.index(max(drawn.shape))
    next_to = spot[:widest] + [(spot[widest] + 1) % drawn.shape[widest]] + spot[widest + 1:]
    return drawn.at[tuple(spot)].set(smallest).at[tuple(next_to)].set(high)


def steps_of(stream_key, shape, pieces, smallest, high):
    factor_of = 1.0
    for dim, parts in pieces:
        steps = jax.random.uniform(jax.random.fold_in(jax.random.fold_in(stream_key, 6), dim), (parts,), jnp.float32, smallest / len(pieces), high / len(pieces))
        factor_of = factor_of * jnp.repeat(jnp.exp(steps), shape[dim] // parts).reshape((-1,) + (1,) * (len(shape) - 1 - dim))
    return factor_of


def noise(rng, extent, scale, reach, cuts=(), kind=jnp.bfloat16):
    drawn = scale * jax.random.normal(rng, extent, jnp.float32)
    if cuts:
        drawn = drawn * steps_of(rng, extent, cuts, -0.22, 0.18)
    return jnp.clip(drawn, -reach, reach).astype(kind)


def setup_inputs(seed: int = 0) -> dict:
    splits = jax.random.split(jax.random.key(seed), 9)
    rhs = draw_rhs(jax.random.fold_in(splits[8], 71), 0)
    schur = draw_schur(jax.random.fold_in(splits[8], 71), 0)
    stiff = jnp.clip(jnp.exp(math.log(100.0) - 4.6051702 * jax.random.uniform(splits[2], (N_GRP, N_SUB, NI), jnp.float32) ** steps_of(splits[2], (N_GRP, N_SUB, NI), ((0, 32), (1, 8)), -0.2, 0.2)), 1.0, 100.0)
    face_index = jax.vmap(lambda own: jax.random.permutation(own, NI))(jax.random.split(splits[3], N_GRP * N_SUB)).reshape((N_GRP, N_SUB, NI)).astype(jnp.int32)
    basis = noise(splits[4], (N_GRP, N_SUB, NI, G1), NI ** -0.5, 0.125, ((0, 32), (1, 8)))
    membership = plant(jax.random.randint(splits[5], (N_GRP, G1), 0, G2), jax.random.fold_in(splits[5], 1), 0, G2 - 1).astype(jnp.int32)
    level1_inv = draw_level1_inv(jax.random.fold_in(splits[8], 71), 0)
    level2_inv = draw_level2_inv(jax.random.fold_in(splits[8], 71), 0)
    return {"rhs": rhs, "schur": schur, "stiff": stiff, "face_index": face_index, "basis": basis, "membership": membership, "level1_inv": level1_inv, "level2_inv": level2_inv}


def incoming_values(values, face_order):
    columns = values.shape[-1]
    face_size = NI // 4
    face_blocks = jnp.take_along_axis(values, face_order[..., None], axis=2).reshape(N_GRP, N_SUB, 4, face_size, columns)
    arrived = jnp.stack([jnp.roll(face_blocks[:, :, 1], 1, axis=1), jnp.roll(face_blocks[:, :, 0], -1, axis=1), jnp.roll(face_blocks[:, :, 3], 1, axis=0), jnp.roll(face_blocks[:, :, 2], -1, axis=0)], axis=2).reshape(N_GRP, N_SUB, NI, columns)
    def place_one(order_row, arrived_row):
        return jnp.zeros_like(arrived_row).at[order_row].set(arrived_row)
    return jax.vmap(jax.vmap(place_one))(face_order, arrived)


def apply_schur(schur, values):
    flat_mats = schur.reshape(N_GRP * N_SUB, NI, NI)
    flat_vals = values.reshape(N_GRP * N_SUB, NI, values.shape[-1])
    def one_product(pair):
        return jnp.dot(pair[0], pair[1].astype(jnp.bfloat16), preferred_element_type=jnp.float32)
    return lax.map(one_product, (flat_mats, flat_vals)).reshape(values.shape)


def reference(rhs, schur, stiff, face_index, basis, membership, level1_inv, level2_inv):
    high = lax.Precision.HIGHEST
    other_stiff = incoming_values(stiff[..., None], face_index)[..., 0]
    weight_col = (stiff / (stiff + other_stiff))[..., None]
    diagonal_part = jnp.diagonal(schur, axis1=2, axis2=3).astype(jnp.float32)[..., None]
    aggregation = (membership[:, None, :] == jnp.arange(G2, dtype=jnp.int32)[None, :, None]).astype(jnp.float32)
    basis_wide = basis.astype(jnp.float32)

    def assemble(values):
        return values + incoming_values(values, face_index)

    def operate(values):
        return assemble(apply_schur(schur, values))

    def inner(first, second):
        return 0.5 * jnp.sum(first * second, axis=(0, 1, 2))

    def precondition(current):
        weighted = weight_col * current
        weighted_bf = weighted.astype(jnp.bfloat16)
        local_fix = weighted / diagonal_part
        for sweep in range(LOCAL_STEPS):
            local_fix = local_fix + (weighted - apply_schur(schur, local_fix)) / diagonal_part
        partial_value = jnp.einsum("gsnk,gsnr->gskr", basis_wide, weighted_bf.astype(jnp.float32), precision=high)
        group_total = jnp.sum(partial_value, axis=1)
        level_two = jnp.einsum("gak,gkr->ar", aggregation, group_total, precision=high)
        solved_two = jnp.dot(level2_inv, level_two, precision=high)
        coarse_value = jnp.einsum("gkl,glr->gkr", level1_inv, group_total, precision=high) + jnp.einsum("gak,ar->gkr", aggregation, solved_two, precision=high)
        coarse_bf = coarse_value.astype(jnp.bfloat16).astype(jnp.float32)
        correction = jnp.einsum("gsnk,gkr->gsnr", basis_wide, coarse_bf, precision=high)
        return assemble(weight_col * (local_fix + correction))

    residual = assemble(rhs)
    solution = jnp.zeros_like(residual)
    z_value = precondition(residual)
    direction = z_value
    r_dot_z = inner(residual, z_value)
    for step in range(ITERS):
        image = operate(direction)
        step_len = r_dot_z / inner(direction, image)
        solution = solution + step_len * direction
        residual = residual - step_len * image
        if step + 1 < ITERS:
            z_value = precondition(residual)
            next_dot = inner(residual, z_value)
            direction = z_value + (next_dot / r_dot_z) * direction
            r_dot_z = next_dot
    return solution, residual
```

```python
import jax
import jax.numpy as jnp
from jax import lax
from jax.sharding import PartitionSpec as P

LOCAL_STEPS = 2
HIGH = lax.Precision.HIGHEST
BF = jnp.bfloat16
F32 = jnp.float32


def passed_along(value, axis, steps):
    count = lax.axis_size(axis)
    pairs = [(source, (source + steps) % count) for source in range(count)]
    return lax.ppermute(value, axis, pairs)


def spread(chunks, axis, groups=None):
    return lax.all_to_all(chunks, axis, 0, 0, axis_index_groups=groups)


def copies(value, count):
    return jnp.broadcast_to(value[None], (count,) + value.shape)


def dot(first, second, contract, precision=None):
    return lax.dot_general(
        first, second, (contract, ((), ())), precision=precision, preferred_element_type=F32
    )


def split(value):
    top = value.astype(BF)
    return jnp.concatenate([top, (value - top.astype(F32)).astype(BF)], axis=1)


def body(rhs, schur, stiff, face_index, basis, membership, level1_inv, level2_inv):
    matrix_in = schur[0, 0]
    order = face_index[0, 0]
    inverse_one = level1_inv[0]
    dofs, cols = rhs.shape[2], rhs.shape[3]
    face = dofs // 4
    coarse = level1_inv.shape[1]
    coarse_two = level2_inv.shape[0]
    n_sub, n_grp = lax.axis_size("sub"), lax.axis_size("grp")
    inner_y = 4 if n_grp % 4 == 0 else 1
    outer_z = n_grp // inner_y
    groups_y = [[z * inner_y + y for y in range(inner_y)] for z in range(outer_z)]
    groups_z = [[z * inner_y + y for z in range(outer_z)] for y in range(inner_y)]
    share = cols // n_sub

    pick = (order[:, None] == jnp.arange(dofs, dtype=jnp.int32)[None, :]).astype(BF)
    rhs_f = rhs[0, 0][order]
    stiff_col = stiff[0, 0][:, None]
    stiff_hi = stiff_col.astype(BF)
    stiff_mid = (stiff_col - stiff_hi.astype(F32)).astype(BF)
    stiff_lo = (stiff_col - stiff_hi.astype(F32) - stiff_mid.astype(F32)).astype(BF)
    stiff_parts = dot(pick, jnp.concatenate([stiff_hi, stiff_mid, stiff_lo], axis=1), ((1,), (0,)))
    stiff_f = stiff_parts[:, 0:1] + stiff_parts[:, 1:2] + stiff_parts[:, 2:3]

    def exchanged(blocks):
        return [
            passed_along(blocks[1], "sub", 1),
            passed_along(blocks[0], "sub", -1),
            passed_along(blocks[3], "grp", 1),
            passed_along(blocks[2], "grp", -1),
        ]

    def incoming(vector):
        return jnp.concatenate(exchanged([vector[k * face : (k + 1) * face] for k in range(4)]), axis=0)

    stiff_rows = face // cols
    blocks = [
        jnp.concatenate(
            [rhs_f[k * face : (k + 1) * face], stiff_f[k * face : (k + 1) * face].reshape(stiff_rows, cols)],
            axis=0,
        )
        for k in range(4)
    ]
    arrived = exchanged(blocks)
    residual0 = rhs_f + jnp.concatenate([block[:face] for block in arrived], axis=0)
    stiff_in = jnp.concatenate([block[face:].reshape(face, 1) for block in arrived], axis=0)
    weight = stiff_f / (stiff_f + stiff_in)

    basis_f = dot(pick, basis[0, 0], ((1,), (0,))).astype(BF)
    half_way = dot(pick, matrix_in, ((1,), (0,))).astype(BF)
    matrix = dot(half_way, pick, ((1,), (1,))).astype(BF)
    row_id = lax.broadcasted_iota(jnp.int32, (dofs, dofs), 0)
    col_id = lax.broadcasted_iota(jnp.int32, (dofs, dofs), 1)
    diagonal = jnp.sum(jnp.where(row_id == col_id, matrix.astype(F32), 0.0), axis=1)[:, None]
    aggregation = (membership[0][None, :] == jnp.arange(coarse_two, dtype=jnp.int32)[:, None]).astype(F32)

    def schur_times(vector):
        return dot(matrix, vector.astype(BF), ((1,), (0,)))

    def schur_times_split(vector):
        both = dot(matrix, split(vector), ((1,), (0,)))
        return both[:, :cols] + both[:, cols:]

    def corrected(weighted, fix):
        for _ in range(LOCAL_STEPS):
            fix = fix + (weighted - schur_times(fix)) / diagonal
        return fix

    def group_sum(partial):
        chunks = partial.reshape(n_sub, share, partial.shape[1])
        return jnp.sum(spread(chunks, "sub"), axis=0)

    def all_groups(value):
        if inner_y > 1:
            value = jnp.sum(spread(copies(value, inner_y), "grp", groups_y), axis=0)
        return jnp.sum(spread(copies(value, outer_z), "grp", groups_z), axis=0)

    def gathered(value):
        return spread(copies(value, n_sub), "sub").reshape(n_sub * share, value.shape[1])

    def level_two_of(group_total):
        return dot(group_total, aggregation, ((1,), (1,)), HIGH)

    def coarse_solve(group_total, level_two):
        solved_two = dot(level_two, level2_inv, ((1,), (1,)), HIGH)
        return dot(group_total, inverse_one, ((1,), (1,)), HIGH) + dot(
            solved_two, aggregation, ((1,), (0,)), HIGH
        )

    def finish(fix, coarse_value):
        correction = dot(basis_f, coarse_value.astype(BF), ((1,), (1,)))
        local_sum = weight * (fix + correction)
        return local_sum + incoming(local_sum)

    weighted = weight * residual0
    total0 = group_sum(dot(weighted.astype(BF), basis_f, ((0,), (0,))))
    two0 = all_groups(level_two_of(total0))
    coarse0 = 2.0 * gathered(0.5 * coarse_solve(total0, two0))
    z0 = finish(corrected(weighted, weighted / diagonal), coarse0)

    product0 = schur_times_split(z0)
    image0 = product0 + incoming(product0)

    dots0 = jnp.stack([0.5 * jnp.sum(residual0 * z0, axis=0), jnp.sum(z0 * product0, axis=0)], axis=1)
    dots0 = jnp.pad(dots0, ((0, 0), (0, 126)))
    both = dot(split(weight * image0), basis_f, ((0,), (0,)))
    mixed = group_sum(jnp.concatenate([both[:cols] + both[cols:], dots0], axis=1))
    total_q, dots = mixed[:, :coarse], mixed[:, coarse:]
    mixed = all_groups(jnp.concatenate([level_two_of(total_q), dots], axis=1))
    two_q, dots = mixed[:, :coarse_two], mixed[:, coarse_two:]
    step0 = dots[:, 0:1] / dots[:, 1:2]
    coarse1 = coarse_solve(total0 - step0 * total_q, two0 - step0 * two_q)
    lane = lax.broadcasted_iota(jnp.int32, dots.shape, 1)
    mixed = lax.optimization_barrier(
        gathered(jnp.concatenate([coarse1, jnp.where(lane == 2, step0, dots)], axis=1))
    )
    rz0, zaz0, step0 = (mixed[:, coarse + k][None, :] for k in range(3))
    coarse1 = mixed[:, :coarse]

    residual1 = residual0 - step0 * image0
    weighted = weight * residual1
    z1 = finish(corrected(weighted, weighted / diagonal), coarse1)
    product1 = schur_times_split(z1)
    dots1 = jnp.stack(
        [
            0.5 * jnp.sum(residual1 * z1, axis=0),
            jnp.sum(z1 * product1, axis=0),
            jnp.sum(z0 * product1, axis=0),
        ],
        axis=0,
    )
    dots1 = jnp.sum(spread(copies(dots1, n_sub), "sub"), axis=0)
    dots1 = jnp.sum(spread(copies(dots1, n_grp), "grp"), axis=0)
    rz1, zaz1, zaz01 = dots1[0:1], dots1[1:2], dots1[2:3]
    image1 = product1 + incoming(product1)
    ratio = rz1 / rz0
    step1 = rz1 / (zaz1 + 2.0 * ratio * zaz01 + ratio * ratio * zaz0)
    solution_f = step0 * z0 + step1 * (z1 + ratio * z0)
    residual_f = residual1 - step1 * (image1 + ratio * image0)
    outs = [jnp.zeros_like(value).at[order].set(value) for value in (solution_f, residual_f)]
    return outs[0][None, None], outs[1][None, None]


def solution(mesh):
    placed = (
        P("grp", "sub", None, None),
        P("grp", "sub", None, None),
        P("grp", "sub", None),
        P("grp", "sub", None),
        P("grp", "sub", None, None),
        P("grp", None),
        P("grp", None, None),
        P(),
    )
    return jax.shard_map(
        body,
        mesh=mesh,
        in_specs=placed,
        out_specs=(P("grp", "sub", None, None), P("grp", "sub", None, None)),
        check_vma=False,
    )
```

```python
import functools

import jax
import jax.numpy as jnp
from jax import lax
from jax.experimental import pallas as pl
from jax.experimental.pallas import tpu as pltpu
from jax.sharding import PartitionSpec as P

LOCAL_STEPS = 2
HIGH = lax.Precision.HIGHEST
BF = jnp.bfloat16
F32 = jnp.float32
LANES = 128
GATHER = 32
CHUNK = 512
VM = pl.BlockSpec(memory_space=pltpu.VMEM)
SM = pl.BlockSpec(memory_space=pltpu.SMEM)


def shape(*dims, kind=F32):
    return jax.ShapeDtypeStruct(dims, kind)


def kernel(body, operands, outs, scratch=(), limit=40, scalars=1, flops=0):
    specs = [SM] * scalars + [VM] * (len(operands) - scalars)
    moved = sum(value.size * value.dtype.itemsize for value in (*operands, *outs))
    return pl.pallas_call(
        body,
        out_shape=list(outs),
        in_specs=specs,
        out_specs=[VM] * len(outs),
        scratch_shapes=list(scratch),
        compiler_params=pltpu.CompilerParams(vmem_limit_bytes=limit << 20),
        cost_estimate=pl.CostEstimate(flops=flops, bytes_accessed=moved, transcendentals=0),
        name=body.func.__name__ if isinstance(body, functools.partial) else body.__name__,
    )(*operands)


def dot(first, second, contract, precision=None):
    return lax.dot_general(
        first, second, (contract, ((), ())), precision=precision, preferred_element_type=F32
    )


def eye():
    return (
        lax.broadcasted_iota(jnp.int32, (LANES, LANES), 0)
        == lax.broadcasted_iota(jnp.int32, (LANES, LANES), 1)
    )


def to_column(row):
    column = jnp.sum(jnp.where(eye(), jnp.broadcast_to(row, (LANES, LANES)), 0.0), axis=1, keepdims=True)
    return jnp.broadcast_to(column, (LANES, LANES))


def to_row(block):
    return jnp.sum(jnp.where(eye(), block, 0.0), axis=0, keepdims=True)


def gather_rows(order, start, count, pairs):
    @pl.loop(0, count // GATHER)
    def _(step):
        base = pl.multiple_of(step * GATHER, GATHER)
        picks = [order[0, start + base + k] for k in range(GATHER)]
        for source, target in pairs:
            target[pl.ds(base, GATHER), :] = jnp.concatenate(
                [source[pl.ds(pick, 1), :] for pick in picks], axis=0
            )


def scatter_rows(order, start, count, pairs):
    @pl.loop(0, count // GATHER)
    def _(step):
        base = pl.multiple_of(step * GATHER, GATHER)
        picks = [order[0, start + base + k] for k in range(GATHER)]
        for source, target in pairs:
            rows = source[pl.ds(base, GATHER), :]
            for k, pick in enumerate(picks):
                target[pl.ds(pick, 1), :] = rows[k : k + 1]


def chunked(rows, work):
    for start in range(0, rows, CHUNK):
        work(pl.ds(start, CHUNK))


def spread_stiff(stiff, target):
    for start in range(0, target.shape[0], LANES):
        target[pl.ds(start, LANES), :] = to_column(stiff[:, pl.ds(start, LANES)])


def split(value):
    top = value.astype(BF)
    return top, (value - top.astype(F32)).astype(BF)


def membership_table(members, levels):
    rows = lax.broadcasted_iota(jnp.int32, (levels, members.shape[1]), 0)
    return (rows == members[...]).astype(F32)


def open_faces(order, rhs, stiff, *rest):
    blocks, (own_stiff, face_stiff) = rest[:4], rest[4:]
    face = rhs.shape[0] // 4
    spread_stiff(stiff, own_stiff)
    for k, block in enumerate(blocks):
        gather_rows(order, k * face, face, [(rhs, block), (own_stiff, face_stiff)])
        block[pl.ds(face, block.shape[0] - face), :] = jnp.concatenate(
            [to_row(face_stiff[pl.ds(t, LANES), :]) for t in range(0, face, LANES)]
            + [jnp.zeros((block.shape[0] - face - face // LANES, LANES), F32)],
            axis=0,
        )


def open_join(order, rhs, stiff, one, two, three, four, basis, residual, weight, weighted, partial, other, face_stiff):
    face = rhs.shape[0] // 4
    for k, block in enumerate((one, two, three, four)):
        for t in range(face // LANES):
            face_stiff[pl.ds(t * LANES, LANES), :] = to_column(block[pl.ds(face + t, 1), :])
        scatter_rows(order, k * face, face, [(block, residual), (face_stiff, other)])
    spread_stiff(stiff, weight)
    residual[...] = rhs[...] + residual[...]
    weight[...] = weight[...] / (weight[...] + other[...])
    weighted[...] = weight[...] * residual[...]
    partial[...] = dot(weighted[...].astype(BF), basis[...], ((0,), (0,)))


def sweeps(matrix, weighted, diagonal, fix, narrow):
    fix[...] = weighted[...] / diagonal[...]
    for _ in range(LOCAL_STEPS):
        narrow[...] = fix[...].astype(BF)

        def work(rows):
            product = dot(matrix[rows, :], narrow[...], ((1,), (0,)))
            fix[rows, :] = fix[rows, :] + (weighted[rows, :] - product) / diagonal[rows, :]

        chunked(matrix.shape[0], work)


def first_fix(matrix, weighted, fix, diagonal, narrow):
    for start in range(0, matrix.shape[0], LANES):
        square = matrix[pl.ds(start, LANES), pl.ds(start, LANES)].astype(F32)
        column = jnp.sum(jnp.where(eye(), square, 0.0), axis=1, keepdims=True)
        diagonal[pl.ds(start, LANES), :] = jnp.broadcast_to(column, (LANES, LANES))
    sweeps(matrix, weighted, diagonal, fix, narrow)


def add_coarse(basis, coarse, weight, fix, local):
    narrow = coarse.astype(BF)

    def work(rows):
        correction = dot(basis[rows, :], narrow, ((1,), (1,)))
        local[rows, :] = weight[rows, :] * (fix[rows, :] + correction)

    chunked(basis.shape[0], work)


def send_faces(order, source, blocks):
    face = source.shape[0] // 4
    for k, block in enumerate(blocks):
        gather_rows(order, k * face, face, [(source, block)])


def first_local(order, weight, fix, basis, coarse, local, *blocks):
    add_coarse(basis, coarse[...], weight, fix, local)
    send_faces(order, local, blocks)


def apply_schur(matrix, vector, product, wide):
    wide[:, :LANES], wide[:, LANES:] = split(vector[...])

    def work(rows):
        both = dot(matrix[rows, :], wide[...], ((1,), (0,)))
        product[rows, :] = both[:, :LANES] + both[:, LANES:]

    chunked(matrix.shape[0], work)


def column_sum(first, second):
    return jnp.sum(first[...] * second[...], axis=0, keepdims=True)


def first_apply(order, matrix, local, residual, one, two, three, four, z_value, product, dots, *rest):
    blocks, wide = rest[:4], rest[4]
    face = local.shape[0] // 4
    for k, block in enumerate((one, two, three, four)):
        scatter_rows(order, k * face, face, [(block, z_value)])
    z_value[...] = local[...] + z_value[...]
    apply_schur(matrix, z_value, product, wide)
    send_faces(order, product, blocks)
    dots[...] = jnp.concatenate(
        [0.5 * column_sum(residual, z_value), column_sum(z_value, product), jnp.zeros((6, LANES), F32)], axis=0
    )


def image_partial(order, product, weight, one, two, three, four, basis, dots, image, payload, wide):
    face = product.shape[0] // 4
    for k, block in enumerate((one, two, three, four)):
        scatter_rows(order, k * face, face, [(block, image)])
    image[...] = product[...] + image[...]
    wide[:, :LANES], wide[:, LANES:] = split(weight[...] * image[...])
    both = dot(wide[...], basis[...], ((0,), (0,)))
    coarse = basis.shape[1]
    payload[:, :coarse] = both[:LANES] + both[LANES:]
    square = jnp.concatenate([dots[...], jnp.zeros((LANES - 8, LANES), F32)], axis=0)
    payload[:, coarse:] = square.T


def group_level(chunks, members, total, copies, *, levels):
    value = jnp.sum(chunks[...], axis=0)
    total[...] = value
    coarse = members.shape[1]
    copies[0, :, :levels] = dot(value[:, :coarse], membership_table(members, levels), ((1,), (1,)), HIGH)
    if value.shape[1] > coarse:
        copies[0, :, levels:] = value[:, coarse:]
    for k in range(1, copies.shape[0]):
        copies[k] = copies[0]


def add_and_copy(chunks, copies):
    value = jnp.sum(chunks[...], axis=0)
    for k in range(copies.shape[0]):
        copies[k] = value


def coarse_solve(total, two, members, inverse_one, inverse_two):
    solved = dot(two, inverse_two[...], ((1,), (1,)), HIGH)
    table = membership_table(members, inverse_two.shape[0])
    return dot(total, inverse_one[...], ((1,), (1,)), HIGH) + dot(solved, table, ((1,), (0,)), HIGH)


def first_coarse(chunks, total, members, inverse_one, inverse_two, two, copies):
    two[...] = jnp.sum(chunks[...], axis=0)
    value = coarse_solve(total[...], two[...], members, inverse_one, inverse_two)
    for k in range(copies.shape[0]):
        copies[k] = value


def second_coarse(chunks, total_q, total, two, members, inverse_one, inverse_two, copies):
    levels, coarse = inverse_two.shape[0], members.shape[1]
    value = jnp.sum(chunks[...], axis=0)
    dots = value[:, levels:]
    step = dots[:, 0:1] / dots[:, 1:2]
    solved = coarse_solve(
        total[...] - step * total_q[:, :coarse], two[...] - step * value[:, :levels], members, inverse_one, inverse_two
    )
    dots = jnp.where(lax.broadcasted_iota(jnp.int32, dots.shape, 1) == 2, step, dots)
    for k in range(copies.shape[0]):
        copies[k, :, :coarse] = solved
        copies[k, :, coarse:] = dots


def second_local(order, matrix, diagonal, weight, basis, residual, image, coarse, residual_out, local, info, *rest):
    blocks, (weighted, fix, narrow) = rest[:4], rest[4:]
    levels = basis.shape[1]
    rows = coarse[:, levels:].T
    info[...] = rows[:8]
    residual_out[...] = residual[...] - rows[2:3] * image[...]
    weighted[...] = weight[...] * residual_out[...]
    sweeps(matrix, weighted, diagonal, fix, narrow)
    add_coarse(basis, coarse[:, :levels], weight, fix, local)
    send_faces(order, local, blocks)


def second_apply(order, matrix, local, residual, z_first, one, two, three, four, z_value, product, copies, *rest):
    blocks, wide = rest[:4], rest[4]
    face = local.shape[0] // 4
    for k, block in enumerate((one, two, three, four)):
        scatter_rows(order, k * face, face, [(block, z_value)])
    z_value[...] = local[...] + z_value[...]
    apply_schur(matrix, z_value, product, wide)
    send_faces(order, product, blocks)
    dots = jnp.concatenate(
        [
            0.5 * column_sum(residual, z_value),
            column_sum(z_value, product),
            column_sum(z_first, product),
            jnp.zeros((5, LANES), F32),
        ],
        axis=0,
    )
    for k in range(copies.shape[0]):
        copies[k] = dots


def last_image(order, product, one, two, three, four, image):
    face = product.shape[0] // 4
    for k, block in enumerate((one, two, three, four)):
        scatter_rows(order, k * face, face, [(block, image)])
    image[...] = product[...] + image[...]


def finish(chunks, info, z_first, z_second, image_first, image_second, residual, solution_out, residual_out):
    dots = jnp.sum(chunks[...], axis=0)
    rz_first, step_first = info[0:1], info[2:3]
    rz = dots[0:1]
    ratio = rz / rz_first
    step = rz / (dots[1:2] + 2.0 * ratio * dots[2:3] + ratio * ratio * info[1:2])
    solution_out[...] = step_first * z_first[...] + step * (z_second[...] + ratio * z_first[...])
    residual_out[...] = residual[...] - step * (image_second[...] + ratio * image_first[...])


def passed_along(value, axis, steps):
    count = lax.axis_size(axis)
    pairs = [(source, (source + steps) % count) for source in range(count)]
    return lax.ppermute(value, axis, pairs)


def exchanged(blocks):
    return [
        passed_along(blocks[1], "sub", 1),
        passed_along(blocks[0], "sub", -1),
        passed_along(blocks[3], "grp", 1),
        passed_along(blocks[2], "grp", -1),
    ]


def spread(chunks, axis, groups=None):
    return lax.all_to_all(chunks, axis, 0, 0, axis_index_groups=groups)


def body(rhs, schur, stiff, face_index, basis, membership, level1_inv, level2_inv):
    matrix, rhs, basis = schur[0, 0], rhs[0, 0], basis[0, 0]
    order, stiff, members, inverse_one = face_index[0], stiff[0], membership, level1_inv[0]
    dofs, cols = rhs.shape
    face = dofs // 4
    coarse, levels = inverse_one.shape[0], level2_inv.shape[0]
    n_sub, n_grp = lax.axis_size("sub"), lax.axis_size("grp")
    inner = 4
    outer = n_grp // inner
    groups_y = [[z * inner + y for y in range(inner)] for z in range(outer)]
    groups_z = [[z * inner + y for z in range(outer)] for y in range(inner)]
    share = cols // n_sub
    vector, block = shape(dofs, cols), shape(face, cols)
    face_rows = face + -(-face // LANES // 8) * 8
    product_flops = 2 * dofs * dofs * cols
    wide, narrow = pltpu.VMEM((dofs, 2 * cols), BF), pltpu.VMEM((dofs, cols), BF)

    blocks = kernel(
        open_faces,
        (order, rhs, stiff),
        [shape(face_rows, cols)] * 4,
        [pltpu.VMEM((dofs, cols), F32), pltpu.VMEM((face, cols), F32)],
    )
    residual0, weight, weighted, partial = kernel(
        open_join,
        (order, rhs, stiff, *exchanged(blocks), basis),
        [vector, vector, vector, shape(cols, coarse)],
        [pltpu.VMEM((dofs, cols), F32), pltpu.VMEM((face, cols), F32)],
    )

    def to_groups(value):
        chunks = spread(value.reshape(n_sub, share, value.shape[1]), "sub")
        width = value.shape[1]
        out = width - coarse + levels
        total, copies = kernel(
            functools.partial(group_level, levels=levels),
            (chunks, members),
            [shape(share, width), shape(inner, share, out)],
            scalars=0,
        )
        chunks = spread(copies, "grp", groups_y)
        (copies,) = kernel(add_and_copy, (chunks,), [shape(outer, share, out)], scalars=0)
        return total, spread(copies, "grp", groups_z)

    def from_groups(copies):
        return spread(copies, "sub").reshape(cols, copies.shape[2])

    total0, chunks = to_groups(partial)
    two0, copies = kernel(
        first_coarse,
        (chunks, total0, members, inverse_one, level2_inv),
        [shape(share, levels), shape(n_sub, share, coarse)],
        scalars=0,
    )
    coarse0 = from_groups(copies)
    fix, diagonal = kernel(
        first_fix, (matrix, weighted), [vector, vector], [narrow], scalars=0, flops=2 * product_flops
    )
    local, *blocks = kernel(first_local, (order, weight, fix, basis, coarse0), [vector] + [block] * 4)

    z0, product0, dots, *blocks = kernel(
        first_apply,
        (order, matrix, local, residual0, *exchanged(blocks)),
        [vector, vector, shape(8, cols)] + [block] * 4,
        [wide],
        flops=product_flops,
    )
    image0, payload = kernel(
        image_partial,
        (order, product0, weight, *exchanged(blocks), basis, dots),
        [vector, shape(cols, coarse + cols)],
        [wide],
    )
    total_q, chunks = to_groups(payload)
    (copies,) = kernel(
        second_coarse,
        (chunks, total_q, total0, two0, members, inverse_one, level2_inv),
        [shape(n_sub, share, coarse + cols)],
        scalars=0,
    )
    coarse1 = from_groups(copies)
    residual1, local, info, *blocks = kernel(
        second_local,
        (order, matrix, diagonal, weight, basis, residual0, image0, coarse1),
        [vector, vector, shape(8, cols)] + [block] * 4,
        [pltpu.VMEM((dofs, cols), F32), pltpu.VMEM((dofs, cols), F32), narrow],
        flops=2 * product_flops,
    )
    z1, product1, copies, *blocks = kernel(
        second_apply,
        (order, matrix, local, residual1, z0, *exchanged(blocks)),
        [vector, vector, shape(n_sub, 8, cols)] + [block] * 4,
        [wide],
        flops=product_flops,
    )
    arrived = exchanged(blocks)
    (copies,) = kernel(add_and_copy, (spread(copies, "sub"),), [shape(n_grp, 8, cols)], scalars=0)
    chunks = spread(copies, "grp")
    (image1,) = kernel(last_image, (order, product1, *arrived), [vector])
    outs = kernel(
        finish, (chunks, info, z0, z1, image0, image1, residual1), [vector, vector], scalars=0
    )
    return outs[0][None, None], outs[1][None, None]


def solution(mesh):
    placed = (
        P("grp", "sub", None, None),
        P("grp", "sub", None, None),
        P("grp", "sub", None),
        P("grp", "sub", None),
        P("grp", "sub", None, None),
        P("grp", None),
        P("grp", None, None),
        P(),
    )
    return jax.shard_map(
        body,
        mesh=mesh,
        in_specs=placed,
        out_specs=(P("grp", "sub", None, None), P("grp", "sub", None, None)),
        check_vma=False,
    )
```

```python
import functools

import jax
import jax.numpy as jnp
from jax import lax
from jax.experimental import pallas as pl
from jax.experimental.pallas import tpu as pltpu
from jax.sharding import PartitionSpec as P

LOCAL_STEPS = 2
HIGH = lax.Precision.HIGHEST
BF = jnp.bfloat16
F32 = jnp.float32
LANES = 128
GATHER = 32
CHUNK = 512
VM = pl.BlockSpec(memory_space=pltpu.VMEM)
SM = pl.BlockSpec(memory_space=pltpu.SMEM)


def shape(*dims, kind=F32):
    return jax.ShapeDtypeStruct(dims, kind)


def kernel(body, operands, outs, scratch=(), limit=10, scalars=1, flops=0, aliases=None):
    specs = [SM] * scalars + [VM] * (len(operands) - scalars)
    moved = sum(value.size * value.dtype.itemsize for value in (*operands, *outs))
    return pl.pallas_call(
        body,
        out_shape=list(outs),
        in_specs=specs,
        out_specs=[VM] * len(outs),
        scratch_shapes=list(scratch),
        input_output_aliases=aliases or {},
        compiler_params=pltpu.CompilerParams(vmem_limit_bytes=limit << 20),
        cost_estimate=pl.CostEstimate(flops=flops, bytes_accessed=moved, transcendentals=0),
        name=body.func.__name__ if isinstance(body, functools.partial) else body.__name__,
    )(*operands)


def dot(first, second, contract, precision=None):
    return lax.dot_general(
        first, second, (contract, ((), ())), precision=precision, preferred_element_type=F32
    )


def eye():
    return (
        lax.broadcasted_iota(jnp.int32, (LANES, LANES), 0)
        == lax.broadcasted_iota(jnp.int32, (LANES, LANES), 1)
    )


def to_column(row):
    column = jnp.sum(jnp.where(eye(), jnp.broadcast_to(row, (LANES, LANES)), 0.0), axis=1, keepdims=True)
    return jnp.broadcast_to(column, (LANES, LANES))


def to_row(block):
    return jnp.sum(jnp.where(eye(), block, 0.0), axis=0, keepdims=True)


def gather_rows(order, start, count, pairs):
    @pl.loop(0, count // GATHER)
    def _(step):
        base = pl.multiple_of(step * GATHER, GATHER)
        picks = [order[0, start + base + k] for k in range(GATHER)]
        for source, target in pairs:
            target[pl.ds(base, GATHER), :] = jnp.concatenate(
                [source[pl.ds(pick, 1), :] for pick in picks], axis=0
            )


def scatter_rows(order, start, count, pairs):
    @pl.loop(0, count // GATHER)
    def _(step):
        base = pl.multiple_of(step * GATHER, GATHER)
        picks = [order[0, start + base + k] for k in range(GATHER)]
        for source, target in pairs:
            rows = source[pl.ds(base, GATHER), :]
            for k, pick in enumerate(picks):
                target[pl.ds(pick, 1), :] = rows[k : k + 1]


def chunked(rows, work):
    for start in range(0, rows, CHUNK):
        work(pl.ds(start, CHUNK))


def spread_stiff(stiff, target):
    for start in range(0, target.shape[0], LANES):
        target[pl.ds(start, LANES), :] = to_column(stiff[:, pl.ds(start, LANES)])


def split(value):
    top = value.astype(BF)
    return top, (value - top.astype(F32)).astype(BF)


def membership_table(members, levels):
    rows = lax.broadcasted_iota(jnp.int32, (levels, members.shape[1]), 0)
    return (rows == members[...]).astype(F32)


def split_partial(weighted, basis, wide):
    wide[:, :LANES], wide[:, LANES:] = split(weighted)
    both = dot(wide[...], basis[...], ((0,), (0,)))
    return both[:LANES] + both[LANES:]


def open_faces(order, rhs, stiff, *rest):
    blocks, (own_stiff, face_stiff) = rest[:4], rest[4:]
    face = rhs.shape[0] // 4
    spread_stiff(stiff, own_stiff)
    for k, block in enumerate(blocks):
        gather_rows(order, k * face, face, [(rhs, block), (own_stiff, face_stiff)])
        block[pl.ds(face, block.shape[0] - face), :] = jnp.concatenate(
            [to_row(face_stiff[pl.ds(t, LANES), :]) for t in range(0, face, LANES)]
            + [jnp.zeros((block.shape[0] - face - face // LANES, LANES), F32)],
            axis=0,
        )


def open_join(order, rhs, stiff, one, two, three, four, basis, residual, weight, weighted, partial, other, face_stiff, wide):
    face = rhs.shape[0] // 4
    for k, block in enumerate((one, two, three, four)):
        for t in range(face // LANES):
            face_stiff[pl.ds(t * LANES, LANES), :] = to_column(block[pl.ds(face + t, 1), :])
        scatter_rows(order, k * face, face, [(block, residual), (face_stiff, other)])
    spread_stiff(stiff, weight)
    residual[...] = rhs[...] + residual[...]
    weight[...] = weight[...] / (weight[...] + other[...])
    weighted[...] = weight[...] * residual[...]
    partial[...] = split_partial(weighted[...], basis, wide)


def sweeps(matrix, weighted, diagonal, fix, wide):
    fix[...] = weighted[...] / diagonal[...]
    for _ in range(LOCAL_STEPS):
        wide[:, :LANES], wide[:, LANES:] = split(fix[...])

        def work(rows):
            both = dot(matrix[rows, :], wide[...], ((1,), (0,)))
            product = both[:, :LANES] + both[:, LANES:]
            fix[rows, :] = fix[rows, :] + (weighted[rows, :] - product) / diagonal[rows, :]

        chunked(matrix.shape[0], work)


def read_diagonal(matrix, diagonal):
    for start in range(0, matrix.shape[0], LANES):
        square = matrix[pl.ds(start, LANES), pl.ds(start, LANES)].astype(F32)
        column = jnp.sum(jnp.where(eye(), square, 0.0), axis=1, keepdims=True)
        diagonal[pl.ds(start, LANES), :] = jnp.broadcast_to(column, (LANES, LANES))


def local_fix(matrix, weighted, diagonal, fix, wide):
    sweeps(matrix, weighted, diagonal, fix, wide)


def add_coarse(basis, coarse, weight, fix, local):
    narrow = coarse.astype(BF)

    def work(rows):
        correction = dot(basis[rows, :], narrow, ((1,), (1,)))
        local[rows, :] = weight[rows, :] * (fix[rows, :] + correction)

    chunked(basis.shape[0], work)


def send_faces(order, source, blocks):
    face = source.shape[0] // 4
    for k, block in enumerate(blocks):
        gather_rows(order, k * face, face, [(source, block)])


def place_sub(order, one, two, target):
    face = one.shape[0]
    for k, block in enumerate((one, two)):
        scatter_rows(order, k * face, face, [(block, target)])


def place_grp(order, blocks, target):
    face = blocks[0].shape[0]
    for k, block in enumerate(blocks):
        scatter_rows(order, (2 + k) * face, face, [(block, target)])


def first_local(order, weight, fix, basis, coarse, local, *blocks):
    add_coarse(basis, coarse[...], weight, fix, local)
    send_faces(order, local, blocks)


def apply_schur(matrix, vector, product, wide):
    wide[:, :LANES], wide[:, LANES:] = split(vector[...])

    def work(rows):
        both = dot(matrix[rows, :], wide[...], ((1,), (0,)))
        product[rows, :] = both[:, :LANES] + both[:, LANES:]

    chunked(matrix.shape[0], work)


def column_sum(first, second):
    return jnp.sum(first[...] * second[...], axis=0, keepdims=True)


def first_apply(order, matrix, local, residual, three, four, placed, z_value, product, dots, *rest):
    blocks, wide = rest[:4], rest[4]
    place_grp(order, (three, four), z_value)
    z_value[...] = local[...] + z_value[...]
    apply_schur(matrix, z_value, product, wide)
    send_faces(order, product, blocks)
    dots[...] = jnp.concatenate(
        [0.5 * column_sum(residual, z_value), column_sum(z_value, product), jnp.zeros((6, LANES), F32)], axis=0
    )


def image_partial(order, product, weight, three, four, placed, basis, dots, image, weighted, payload, wide):
    place_grp(order, (three, four), image)
    image[...] = product[...] + image[...]
    weighted[...] = weight[...] * image[...]
    coarse = basis.shape[1]
    payload[:, :coarse] = split_partial(weighted[...], basis, wide)
    square = jnp.concatenate([dots[...], jnp.zeros((LANES - 8, LANES), F32)], axis=0)
    payload[:, coarse:] = square.T


def group_level(chunks, members, total, part, *, levels):
    value = jnp.sum(chunks[...], axis=0)
    total[...] = value
    coarse = members.shape[1]
    part[:, :levels] = dot(value[:, :coarse], membership_table(members, levels), ((1,), (1,)), HIGH)
    if value.shape[1] > coarse:
        part[:, levels:] = value[:, coarse:]


def add_and_copy(*refs):
    value = refs[0][...]
    for other in refs[1:-1]:
        value = value + other[...]
    for k in range(refs[-1].shape[0]):
        refs[-1][k] = value


def coarse_solve(total, two, members, inverse_one, inverse_two):
    solved = dot(two, inverse_two[...], ((1,), (1,)), HIGH)
    table = membership_table(members, inverse_two.shape[0])
    return dot(total, inverse_one[...], ((1,), (1,)), HIGH) + dot(solved, table, ((1,), (0,)), HIGH)


def first_coarse(chunks, total, members, inverse_one, inverse_two, two, copies):
    two[...] = jnp.sum(chunks[...], axis=0)
    value = coarse_solve(total[...], two[...], members, inverse_one, inverse_two)
    for k in range(copies.shape[0]):
        copies[k] = value


def second_coarse(chunks, total_q, total, two, members, inverse_one, inverse_two, copies):
    levels, coarse = inverse_two.shape[0], members.shape[1]
    value = jnp.sum(chunks[...], axis=0)
    dots = value[:, levels:]
    step = dots[:, 0:1] / dots[:, 1:2]
    solved = coarse_solve(
        total[...] - step * total_q[:, :coarse], two[...] - step * value[:, :levels], members, inverse_one, inverse_two
    )
    dots = jnp.where(lax.broadcasted_iota(jnp.int32, dots.shape, 1) == 2, step, dots)
    for k in range(copies.shape[0]):
        copies[k, :, :coarse] = solved
        copies[k, :, coarse:] = dots


def second_local(order, weight, basis, residual, image, fix_first, fix_image, coarse, residual_out, local, info, *rest):
    blocks, fix = rest[:4], rest[4]
    levels = basis.shape[1]
    rows = coarse[:, levels:].T
    info[...] = rows[:8]
    fix[...] = fix_first[...] - rows[2:3] * fix_image[...]
    add_coarse(basis, coarse[:, :levels], weight, fix, local)
    residual_out[...] = residual[...] - rows[2:3] * image[...]
    send_faces(order, local, blocks)


def second_apply(order, matrix, local, residual, z_first, three, four, placed, z_value, product, dots, *rest):
    blocks, wide = rest[:4], rest[4]
    place_grp(order, (three, four), z_value)
    z_value[...] = local[...] + z_value[...]
    apply_schur(matrix, z_value, product, wide)
    send_faces(order, product, blocks)
    dots[...] = jnp.concatenate(
        [
            0.5 * column_sum(residual, z_value),
            column_sum(z_value, product),
            column_sum(z_first, product),
            jnp.zeros((5, LANES), F32),
        ],
        axis=0,
    )


def last_image(order, product, three, four, placed, image):
    place_grp(order, (three, four), image)
    image[...] = product[...] + image[...]


def finish(chunks, info, z_first, z_second, image_first, image_second, residual, solution_out, residual_out):
    dots = jnp.sum(chunks[...], axis=0)
    rz_first, step_first = info[0:1], info[2:3]
    rz = dots[0:1]
    ratio = rz / rz_first
    step = rz / (dots[1:2] + 2.0 * ratio * dots[2:3] + ratio * ratio * info[1:2])
    solution_out[...] = step_first * z_first[...] + step * (z_second[...] + ratio * z_first[...])
    residual_out[...] = residual[...] - step * (image_second[...] + ratio * image_first[...])


def passed_along(value, axis, steps):
    count = lax.axis_size(axis)
    pairs = [(source, (source + steps) % count) for source in range(count)]
    return lax.ppermute(value, axis, pairs)


def turned(value, step, inner):
    pairs = [(k, k // inner * inner + (k + step) % inner) for k in range(lax.axis_size("grp"))]
    return lax.ppermute(value, "grp", pairs)


def exchanged(blocks):
    return [
        passed_along(blocks[1], "sub", 1),
        passed_along(blocks[0], "sub", -1),
        passed_along(blocks[3], "grp", 1),
        passed_along(blocks[2], "grp", -1),
    ]


def spread(chunks, axis, groups=None):
    return lax.all_to_all(chunks, axis, 0, 0, axis_index_groups=groups)


def body(rhs, schur, stiff, face_index, basis, membership, level1_inv, level2_inv):
    matrix, rhs, basis = schur[0, 0], rhs[0, 0], basis[0, 0]
    order, stiff, members, inverse_one = face_index[0], stiff[0], membership, level1_inv[0]
    dofs, cols = rhs.shape
    face = dofs // 4
    coarse, levels = inverse_one.shape[0], level2_inv.shape[0]
    n_sub, n_grp = lax.axis_size("sub"), lax.axis_size("grp")
    inner = 4
    outer = n_grp // inner
    groups_z = [[z * inner + y for z in range(outer)] for y in range(inner)]
    share = cols // n_sub
    vector, block = shape(dofs, cols), shape(face, cols)
    face_rows = face + -(-face // LANES // 8) * 8
    product_flops = 2 * dofs * dofs * 2 * cols
    wide = pltpu.VMEM((dofs, 2 * cols), BF)

    def swap(blocks):
        one, two, three, four = exchanged(blocks)
        (placed,) = kernel(place_sub, (order, one, two), [vector])
        return three, four, placed

    blocks = kernel(
        open_faces,
        (order, rhs, stiff),
        [shape(face_rows, cols)] * 4,
        [pltpu.VMEM((dofs, cols), F32), pltpu.VMEM((face, cols), F32)],
    )
    first, matrix = lax.optimization_barrier((blocks[0], matrix))
    (diagonal,) = kernel(read_diagonal, (matrix,), [vector], scalars=0)
    arrived = exchanged([first, *blocks[1:]])
    *arrived, diagonal = lax.optimization_barrier((*arrived, diagonal))
    residual0, weight, weighted, partial = kernel(
        open_join,
        (order, rhs, stiff, *arrived, basis),
        [vector, vector, vector, shape(cols, coarse)],
        [pltpu.VMEM((dofs, cols), F32), pltpu.VMEM((face, cols), F32), wide],
    )

    def to_groups(value, weighted):
        chunks = spread(value.reshape(n_sub, share, value.shape[1]), "sub")
        width = value.shape[1]
        out = width - coarse + levels
        total, part = kernel(
            functools.partial(group_level, levels=levels),
            (chunks, members),
            [shape(share, width), shape(share, out)],
            scalars=0,
        )
        part, weighted = lax.optimization_barrier((part, weighted))
        others = [turned(part, step, inner) for step in range(1, inner)]
        (fix,) = kernel(
            local_fix, (matrix, weighted, diagonal), [vector], [wide], scalars=0, flops=2 * product_flops
        )
        *others, fix = lax.optimization_barrier((*others, fix))
        (copies,) = kernel(add_and_copy, (part, *others), [shape(outer, share, out)], scalars=0)
        return total, spread(copies, "grp", groups_z), fix

    def from_groups(copies):
        return spread(copies, "sub").reshape(cols, copies.shape[2])

    total0, chunks, fix0 = to_groups(partial, weighted)
    two0, copies = kernel(
        first_coarse,
        (chunks, total0, members, inverse_one, level2_inv),
        [shape(share, levels), shape(n_sub, share, coarse)],
        scalars=0,
    )
    coarse0 = from_groups(copies)
    local, *blocks = kernel(first_local, (order, weight, fix0, basis, coarse0), [vector] + [block] * 4)

    z0, product0, dots, *blocks = kernel(
        first_apply,
        (order, matrix, local, residual0, *swap(blocks)),
        [vector, vector, shape(8, cols)] + [block] * 4,
        [wide],
        flops=product_flops,
        aliases={6: 0},
    )
    image0, weighted, payload = kernel(
        image_partial,
        (order, product0, weight, *swap(blocks), basis, dots),
        [vector, vector, shape(cols, coarse + cols)],
        [wide],
        aliases={5: 0},
    )
    total_q, chunks, fix_image = to_groups(payload, weighted)
    (copies,) = kernel(
        second_coarse,
        (chunks, total_q, total0, two0, members, inverse_one, level2_inv),
        [shape(n_sub, share, coarse + cols)],
        scalars=0,
    )
    coarse1 = from_groups(copies)
    residual1, local, info, *blocks = kernel(
        second_local,
        (order, weight, basis, residual0, image0, fix0, fix_image, coarse1),
        [vector, vector, shape(8, cols)] + [block] * 4,
        [pltpu.VMEM((dofs, cols), F32)],
    )
    z1, product1, dots, *blocks = kernel(
        second_apply,
        (order, matrix, local, residual1, z0, *swap(blocks)),
        [vector, vector, shape(8, cols)] + [block] * 4,
        [wide],
        flops=product_flops,
        aliases={7: 0},
    )
    arrived = swap(blocks)
    for mask in (1 << k for k in range(n_sub.bit_length() - 1)):
        dots = dots + lax.ppermute(dots, "sub", [(k, k ^ mask) for k in range(n_sub)])
    (image1,) = kernel(last_image, (order, product1, *arrived), [vector], aliases={4: 0})
    dots, image1 = lax.optimization_barrier((dots, image1))
    (copies,) = kernel(add_and_copy, (dots,), [shape(n_grp, 8, cols)], scalars=0)
    chunks = spread(copies, "grp")
    outs = kernel(
        finish, (chunks, info, z0, z1, image0, image1, residual1), [vector, vector], scalars=0
    )
    return outs[0][None, None], outs[1][None, None]


def solution(mesh):
    placed = (
        P("grp", "sub", None, None),
        P("grp", "sub", None, None),
        P("grp", "sub", None),
        P("grp", "sub", None),
        P("grp", "sub", None, None),
        P("grp", None),
        P("grp", None, None),
        P(),
    )
    return jax.shard_map(
        body,
        mesh=mesh,
        in_specs=placed,
        out_specs=(P("grp", "sub", None, None), P("grp", "sub", None, None)),
        check_vma=False,
    )
```

```python
import functools

import jax
import jax.numpy as jnp
from jax import lax
from jax.experimental import pallas as pl
from jax.experimental.pallas import tpu as pltpu
from jax.sharding import PartitionSpec as P

LOCAL_STEPS = 2
HIGH = lax.Precision.HIGHEST
BF = jnp.bfloat16
F32 = jnp.float32
LANES = 128
GATHER = 32
CHUNK = 512
VM = pl.BlockSpec(memory_space=pltpu.VMEM)
SM = pl.BlockSpec(memory_space=pltpu.SMEM)
HB = pl.BlockSpec(memory_space=pltpu.HBM)


def shape(*dims, kind=F32):
    return jax.ShapeDtypeStruct(dims, kind)


def kernel(body, operands, outs, scratch=(), limit=10, scalars=1, flops=0, aliases=None, specs=None):
    specs = specs or [SM] * scalars + [VM] * (len(operands) - scalars)
    moved = sum(value.size * value.dtype.itemsize for value in (*operands, *outs))
    return pl.pallas_call(
        body,
        out_shape=list(outs),
        in_specs=specs,
        out_specs=[VM] * len(outs),
        scratch_shapes=list(scratch),
        input_output_aliases=aliases or {},
        compiler_params=pltpu.CompilerParams(vmem_limit_bytes=limit << 20),
        cost_estimate=pl.CostEstimate(flops=flops, bytes_accessed=moved, transcendentals=0),
        name=body.func.__name__ if isinstance(body, functools.partial) else body.__name__,
    )(*operands)


def dot(first, second, contract, precision=None):
    return lax.dot_general(
        first, second, (contract, ((), ())), precision=precision, preferred_element_type=F32
    )


def eye():
    return (
        lax.broadcasted_iota(jnp.int32, (LANES, LANES), 0)
        == lax.broadcasted_iota(jnp.int32, (LANES, LANES), 1)
    )


def to_column(row):
    column = jnp.sum(jnp.where(eye(), jnp.broadcast_to(row, (LANES, LANES)), 0.0), axis=1, keepdims=True)
    return jnp.broadcast_to(column, (LANES, LANES))


def to_row(block):
    return jnp.sum(jnp.where(eye(), block, 0.0), axis=0, keepdims=True)


def gather_rows(order, start, count, pairs):
    @pl.loop(0, count // GATHER)
    def _(step):
        base = pl.multiple_of(step * GATHER, GATHER)
        picks = [order[0, start + base + k] for k in range(GATHER)]
        for source, target in pairs:
            target[pl.ds(base, GATHER), :] = jnp.concatenate(
                [source[pl.ds(pick, 1), :] for pick in picks], axis=0
            )


def scatter_rows(order, start, count, pairs):
    @pl.loop(0, count // GATHER)
    def _(step):
        base = pl.multiple_of(step * GATHER, GATHER)
        picks = [order[0, start + base + k] for k in range(GATHER)]
        for source, target in pairs:
            rows = source[pl.ds(base, GATHER), :]
            for k, pick in enumerate(picks):
                target[pl.ds(pick, 1), :] = rows[k : k + 1]


def chunked(rows, work):
    for start in range(0, rows, CHUNK):
        work(pl.ds(start, CHUNK))


def spread_stiff(stiff, target):
    for start in range(0, target.shape[0], LANES):
        target[pl.ds(start, LANES), :] = to_column(stiff[:, pl.ds(start, LANES)])


def split(value):
    top = value.astype(BF)
    return top, (value - top.astype(F32)).astype(BF)


def membership_table(members, levels):
    rows = lax.broadcasted_iota(jnp.int32, (levels, members.shape[1]), 0)
    return (rows == members[...]).astype(F32)


def split_partial(weighted, basis, wide):
    wide[:, :LANES], wide[:, LANES:] = split(weighted)
    both = dot(wide[...], basis[...], ((0,), (0,)))
    return both[:LANES] + both[LANES:]


def pack(value, dots):
    return jnp.concatenate([value[:, k : k + LANES] for k in range(0, value.shape[1], LANES)] + [dots], axis=0)


def unpack(rows, share):
    parts = [rows[k : k + share] for k in range(0, rows.shape[0] - 8, share)]
    return jnp.concatenate(parts, axis=1), rows[rows.shape[0] - 8 :]


def open_faces(order_far, rhs_far, stiff_far, *rest):
    blocks, (order, rhs, stiff, own_stiff, face_stiff, sems) = rest[:4], rest[4:]
    fetches = [
        pltpu.make_async_copy(source, target, sems.at[k])
        for k, (source, target) in enumerate(((order_far, order), (rhs_far, rhs), (stiff_far, stiff)))
    ]
    for fetch in fetches:
        fetch.start()
    face = rhs.shape[0] // 4
    fetches[2].wait()
    spread_stiff(stiff, own_stiff)
    fetches[0].wait()
    fetches[1].wait()
    for k, block in enumerate(blocks):
        gather_rows(order, k * face, face, [(rhs, block), (own_stiff, face_stiff)])
        block[pl.ds(face, block.shape[0] - face), :] = jnp.concatenate(
            [to_row(face_stiff[pl.ds(t, LANES), :]) for t in range(0, face, LANES)]
            + [jnp.zeros((block.shape[0] - face - face // LANES, LANES), F32)],
            axis=0,
        )


def open_place(order, start, blocks, face, residual, other, face_stiff):
    for k, block in enumerate(blocks):
        for t in range(face // LANES):
            face_stiff[pl.ds(t * LANES, LANES), :] = to_column(block[pl.ds(face + t, 1), :])
        scatter_rows(order, start + k * face, face, [(block, residual), (face_stiff, other)])


def open_sub(order, one, two, residual, other, face_stiff):
    open_place(order, 0, (one, two), face_stiff.shape[0], residual, other, face_stiff)


def open_join(
    order, rhs, stiff, three, four, basis, placed, placed_stiff, residual, other, weight, weighted, partial, face_stiff, wide
):
    face = face_stiff.shape[0]
    open_place(order, 2 * face, (three, four), face, residual, other, face_stiff)
    spread_stiff(stiff, weight)
    residual[...] = rhs[...] + residual[...]
    weight[...] = weight[...] / (weight[...] + other[...])
    weighted[...] = weight[...] * residual[...]
    partial[...] = split_partial(weighted[...], basis, wide)


def sweeps(matrix, weighted, diagonal, fix, wide):
    fix[...] = weighted[...] / diagonal[...]
    for _ in range(LOCAL_STEPS):
        wide[:, :LANES], wide[:, LANES:] = split(fix[...])

        def work(rows):
            both = dot(matrix[rows, :], wide[...], ((1,), (0,)))
            product = both[:, :LANES] + both[:, LANES:]
            fix[rows, :] = fix[rows, :] + (weighted[rows, :] - product) / diagonal[rows, :]

        chunked(matrix.shape[0], work)


def read_diagonal(matrix, diagonal):
    for start in range(0, matrix.shape[0], LANES):
        square = matrix[pl.ds(start, LANES), pl.ds(start, LANES)].astype(F32)
        column = jnp.sum(jnp.where(eye(), square, 0.0), axis=1, keepdims=True)
        diagonal[pl.ds(start, LANES), :] = jnp.broadcast_to(column, (LANES, LANES))


def local_fix(matrix, weighted, diagonal, fix, wide):
    sweeps(matrix, weighted, diagonal, fix, wide)


def add_coarse(basis, coarse, weight, fix, local):
    narrow = coarse.astype(BF)

    def work(rows):
        correction = dot(basis[rows, :], narrow, ((1,), (1,)))
        local[rows, :] = weight[rows, :] * (fix[rows, :] + correction)

    chunked(basis.shape[0], work)


def send_grp(order, source, blocks):
    face = source.shape[0] // 4
    for k, block in enumerate(blocks):
        gather_rows(order, (2 + k) * face, face, [(source, block)])


def send_sub(order, source, *blocks):
    face = source.shape[0] // 4
    for k, block in enumerate(blocks):
        gather_rows(order, k * face, face, [(source, block)])


def place_sub(order, blocks, target):
    face = blocks[0].shape[0]
    for k, block in enumerate(blocks):
        scatter_rows(order, k * face, face, [(block, target)])


def place_grp(order, three, four, target):
    face = three.shape[0]
    for k, block in enumerate((three, four)):
        scatter_rows(order, (2 + k) * face, face, [(block, target)])


def first_local(order, weight, fix, basis, coarse, local, *blocks):
    add_coarse(basis, coarse[...], weight, fix, local)
    send_grp(order, local, blocks)


def apply_schur(matrix, vector, product, wide):
    wide[:, :LANES], wide[:, LANES:] = split(vector[...])

    def work(rows):
        both = dot(matrix[rows, :], wide[...], ((1,), (0,)))
        product[rows, :] = both[:, :LANES] + both[:, LANES:]

    chunked(matrix.shape[0], work)


def column_sum(first, second):
    return jnp.sum(first[...] * second[...], axis=0, keepdims=True)


def first_apply(order, matrix, local, residual, one, two, placed, z_value, product, dots, *rest):
    blocks, wide = rest[:2], rest[2]
    place_sub(order, (one, two), z_value)
    z_value[...] = local[...] + z_value[...]
    apply_schur(matrix, z_value, product, wide)
    send_grp(order, product, blocks)
    dots[...] = jnp.concatenate(
        [0.5 * column_sum(residual, z_value), column_sum(z_value, product), jnp.zeros((6, LANES), F32)], axis=0
    )


def image_partial(order, product, weight, one, two, placed, basis, dots, image, weighted, payload, wide):
    place_sub(order, (one, two), image)
    image[...] = product[...] + image[...]
    weighted[...] = weight[...] * image[...]
    value = split_partial(weighted[...], basis, wide)
    share = value.shape[0] // payload.shape[0]
    for k in range(payload.shape[0]):
        payload[k] = pack(value[k * share : (k + 1) * share], dots[...])


def first_groups(chunks, members, total, part, *, levels):
    total[...] = jnp.sum(chunks[...], axis=0)
    part[...] = dot(total[...], membership_table(members, levels), ((1,), (1,)), HIGH)


def second_groups(chunks, members, total, part, *, levels):
    total[...], dots = unpack(jnp.sum(chunks[...], axis=0), total.shape[0])
    part[...] = pack(dot(total[...], membership_table(members, levels), ((1,), (1,)), HIGH), dots)


def copy_row(*refs):
    *parts, copies = refs
    dots = parts[0][...]
    for other in parts[1:]:
        dots = dots + other[...]
    row = jnp.concatenate([dots[k : k + 1] for k in range(3)], axis=1)
    for k in range(copies.shape[0]):
        copies[k] = row


def add_and_copy(*refs):
    value = refs[0][...]
    for other in refs[1:-1]:
        value = value + other[...]
    for k in range(refs[-1].shape[0]):
        refs[-1][k] = value


def coarse_solve(total, two, members, inverse_one, inverse_two):
    solved = dot(two, inverse_two[...], ((1,), (1,)), HIGH)
    table = membership_table(members, inverse_two.shape[0])
    return dot(total, inverse_one[...], ((1,), (1,)), HIGH) + dot(solved, table, ((1,), (0,)), HIGH)


def first_coarse(chunks, total, members, inverse_one, inverse_two, two, copies):
    two[...] = jnp.sum(chunks[...], axis=0)
    value = coarse_solve(total[...], two[...], members, inverse_one, inverse_two)
    for k in range(copies.shape[0]):
        copies[k] = value


def second_coarse(chunks, total_q, total, two, members, inverse_one, inverse_two, copies, info, column):
    share = total.shape[0]
    two_q, dots = unpack(jnp.sum(chunks[...], axis=0), share)
    step = dots[0:1] / dots[1:2]
    info[...] = jnp.concatenate([dots[0:2], step, dots[3:]], axis=0)
    column[...] = to_column(step)
    mine = column[pl.ds(pl.multiple_of(lax.axis_index("sub") * share, 8), share), :][:, 0:1]
    solved = coarse_solve(
        total[...] - mine * total_q[...], two[...] - mine * two_q, members, inverse_one, inverse_two
    )
    for k in range(copies.shape[0]):
        copies[k] = solved


def second_local(order, weight, basis, residual, image, fix_first, fix_image, coarse, info, residual_out, local, *rest):
    blocks, fix = rest[:2], rest[2]
    step = info[2:3]
    fix[...] = fix_first[...] - step * fix_image[...]
    add_coarse(basis, coarse[...], weight, fix, local)
    residual_out[...] = residual[...] - step * image[...]
    send_grp(order, local, blocks)


def second_apply(order, matrix, local, residual, z_first, one, two, placed, z_value, product, dots, *rest):
    blocks, wide = rest[:2], rest[2]
    place_sub(order, (one, two), z_value)
    z_value[...] = local[...] + z_value[...]
    apply_schur(matrix, z_value, product, wide)
    send_grp(order, product, blocks)
    dots[...] = jnp.concatenate(
        [
            0.5 * column_sum(residual, z_value),
            column_sum(z_value, product),
            column_sum(z_first, product),
            jnp.zeros((5, LANES), F32),
        ],
        axis=0,
    )


def last_image(order, product, one, two, placed, image):
    place_sub(order, (one, two), image)
    image[...] = product[...] + image[...]


def finish(chunks, info, z_first, z_second, image_first, image_second, residual, solution_out, residual_out):
    dots = jnp.sum(chunks[...], axis=0)
    rz_first, step_first = info[0:1], info[2:3]
    rz, zaz, zaz_first = (dots[:, k * LANES : (k + 1) * LANES] for k in range(3))
    ratio = rz / rz_first
    step = rz / (zaz + 2.0 * ratio * zaz_first + ratio * ratio * info[1:2])
    solution_out[...] = step_first * z_first[...] + step * (z_second[...] + ratio * z_first[...])
    residual_out[...] = residual[...] - step * (image_second[...] + ratio * image_first[...])


def passed_along(value, axis, steps):
    count = lax.axis_size(axis)
    pairs = [(source, (source + steps) % count) for source in range(count)]
    return lax.ppermute(value, axis, pairs)


def turned(value, step, inner):
    pairs = [(k, k // inner * inner + (k + step) % inner) for k in range(lax.axis_size("grp"))]
    return lax.ppermute(value, "grp", pairs)


def exchanged(blocks):
    return [
        passed_along(blocks[1], "sub", 1),
        passed_along(blocks[0], "sub", -1),
        passed_along(blocks[3], "grp", 1),
        passed_along(blocks[2], "grp", -1),
    ]


def spread(chunks, axis, groups=None):
    return lax.all_to_all(chunks, axis, 0, 0, axis_index_groups=groups)


def body(rhs, schur, stiff, face_index, basis, membership, level1_inv, level2_inv):
    matrix, rhs, basis = schur[0, 0], rhs[0, 0], basis[0, 0]
    order, stiff, members, inverse_one = face_index[0], stiff[0], membership, level1_inv[0]
    dofs, cols = rhs.shape
    face = dofs // 4
    coarse, levels = inverse_one.shape[0], level2_inv.shape[0]
    n_sub, n_grp = lax.axis_size("sub"), lax.axis_size("grp")
    inner = 4
    outer = n_grp // inner
    groups_z = [[z * inner + y for z in range(outer)] for y in range(inner)]
    share = cols // n_sub
    vector, block = shape(dofs, cols), shape(face, cols)
    face_rows = face + -(-face // LANES // 8) * 8
    product_flops = 2 * dofs * dofs * 2 * cols
    wide = pltpu.VMEM((dofs, 2 * cols), BF)

    def swap(source, toward_grp):
        three = passed_along(toward_grp[1], "grp", 1)
        four = passed_along(toward_grp[0], "grp", -1)
        first, second = kernel(send_sub, (order, source), [block] * 2)
        one = passed_along(second, "sub", 1)
        two = passed_along(first, "sub", -1)
        (placed,) = kernel(place_grp, (order, three, four), [vector])
        return one, two, placed

    blocks = kernel(
        open_faces,
        (order, rhs, stiff),
        [shape(face_rows, cols)] * 4,
        [
            pltpu.SMEM((1, dofs), jnp.int32),
            pltpu.VMEM((dofs, cols), F32),
            pltpu.VMEM((1, dofs), F32),
            pltpu.VMEM((dofs, cols), F32),
            pltpu.VMEM((face, cols), F32),
            pltpu.SemaphoreType.DMA((3,)),
        ],
        specs=[HB] * 3,
        limit=60,
    )
    first, matrix = lax.optimization_barrier((blocks[0], matrix))
    (diagonal,) = kernel(read_diagonal, (matrix,), [vector], scalars=0)
    one, two, three, four = exchanged([first, *blocks[1:]])
    placed = kernel(open_sub, (order, one, two), [vector, vector], [pltpu.VMEM((face, cols), F32)])
    three, four, diagonal = lax.optimization_barrier((three, four, diagonal))
    residual0, _, weight, weighted, partial = kernel(
        open_join,
        (order, rhs, stiff, three, four, basis, *placed),
        [vector] * 4 + [shape(cols, coarse)],
        [pltpu.VMEM((face, cols), F32), wide],
        aliases={6: 0, 7: 1},
    )

    def to_groups(body, chunks, weighted):
        chunks = spread(chunks, "sub")
        part_shape = chunks.shape[1:] if chunks.shape[2] == LANES else (share, levels)
        total, part = kernel(
            functools.partial(body, levels=levels),
            (chunks, members),
            [shape(share, coarse), shape(*part_shape)],
            scalars=0,
        )
        part, weighted = lax.optimization_barrier((part, weighted))
        others = [turned(part, step, inner) for step in range(1, inner)]
        (fix,) = kernel(
            local_fix, (matrix, weighted, diagonal), [vector], [wide], scalars=0, flops=2 * product_flops
        )
        *others, fix = lax.optimization_barrier((*others, fix))
        (copies,) = kernel(add_and_copy, (part, *others), [shape(outer, *part_shape)], scalars=0)
        return total, spread(copies, "grp", groups_z), fix

    def from_groups(copies):
        return spread(copies, "sub").reshape(cols, copies.shape[2])

    total0, chunks, fix0 = to_groups(first_groups, partial.reshape(n_sub, share, coarse), weighted)
    two0, copies = kernel(
        first_coarse,
        (chunks, total0, members, inverse_one, level2_inv),
        [shape(share, levels), shape(n_sub, share, coarse)],
        scalars=0,
    )
    coarse0 = from_groups(copies)
    local, *blocks = kernel(first_local, (order, weight, fix0, basis, coarse0), [vector] + [block] * 2)

    z0, product0, dots, *blocks = kernel(
        first_apply,
        (order, matrix, local, residual0, *swap(local, blocks)),
        [vector, vector, shape(8, cols)] + [block] * 2,
        [wide],
        flops=product_flops,
        aliases={6: 0},
    )
    image0, weighted, payload = kernel(
        image_partial,
        (order, product0, weight, *swap(product0, blocks), basis, dots),
        [vector, vector, shape(n_sub, share * coarse // LANES + 8, LANES)],
        [wide],
        aliases={5: 0},
    )
    total_q, chunks, fix_image = to_groups(second_groups, payload, weighted)
    copies, info = kernel(
        second_coarse,
        (chunks, total_q, total0, two0, members, inverse_one, level2_inv),
        [shape(n_sub, share, coarse), shape(8, cols)],
        [pltpu.VMEM((LANES, LANES), F32)],
        scalars=0,
    )
    coarse1 = from_groups(copies)
    residual1, local, *blocks = kernel(
        second_local,
        (order, weight, basis, residual0, image0, fix0, fix_image, coarse1, info),
        [vector, vector] + [block] * 2,
        [pltpu.VMEM((dofs, cols), F32)],
    )
    z1, product1, dots, *blocks = kernel(
        second_apply,
        (order, matrix, local, residual1, z0, *swap(local, blocks)),
        [vector, vector, shape(8, cols)] + [block] * 2,
        [wide],
        flops=product_flops,
        aliases={7: 0},
    )
    dots = dots + lax.ppermute(dots, "sub", [(k, k ^ 1) for k in range(n_sub)])
    blocks[0], dots = lax.optimization_barrier((blocks[0], dots))
    dots = [dots] + [passed_along(dots, "sub", step) for step in range(2, n_sub, 2)]
    arrived = swap(product1, blocks)
    (image1,) = kernel(last_image, (order, product1, *arrived), [vector], aliases={4: 0})
    *dots, image1 = lax.optimization_barrier((*dots, image1))
    (copies,) = kernel(copy_row, dots, [shape(n_grp, 1, 3 * cols)], scalars=0)
    chunks = spread(copies, "grp")
    outs = kernel(
        finish, (chunks, info, z0, z1, image0, image1, residual1), [vector, vector], scalars=0
    )
    return outs[0][None, None], outs[1][None, None]


def solution(mesh):
    placed = (
        P("grp", "sub", None, None),
        P("grp", "sub", None, None),
        P("grp", "sub", None),
        P("grp", "sub", None),
        P("grp", "sub", None, None),
        P("grp", None),
        P("grp", None, None),
        P(),
    )
    return jax.shard_map(
        body,
        mesh=mesh,
        in_specs=placed,
        out_specs=(P("grp", "sub", None, None), P("grp", "sub", None, None)),
        check_vma=False,
    )
```

```python
import functools

import jax
import jax.numpy as jnp
from jax import lax
from jax.experimental import pallas as pl
from jax.experimental.pallas import tpu as pltpu
from jax.sharding import PartitionSpec as P

LOCAL_STEPS = 2
HIGH = lax.Precision.HIGHEST
BF = jnp.bfloat16
F32 = jnp.float32
LANES = 128
GATHER = 64
CHUNK = 256
VM = pl.BlockSpec(memory_space=pltpu.VMEM)
SM = pl.BlockSpec(memory_space=pltpu.SMEM)
HB = pl.BlockSpec(memory_space=pltpu.HBM)


def shape(*dims, kind=F32):
    return jax.ShapeDtypeStruct(dims, kind)


def kernel(body, operands, outs, scratch=(), limit=10, scalars=1, flops=0, aliases=None, specs=None):
    specs = specs or [SM] * scalars + [VM] * (len(operands) - scalars)
    moved = sum(value.size * value.dtype.itemsize for value in (*operands, *outs))
    return pl.pallas_call(
        body,
        out_shape=list(outs),
        in_specs=specs,
        out_specs=[VM] * len(outs),
        scratch_shapes=list(scratch),
        input_output_aliases=aliases or {},
        compiler_params=pltpu.CompilerParams(vmem_limit_bytes=limit << 20),
        cost_estimate=pl.CostEstimate(flops=flops, bytes_accessed=moved, transcendentals=0),
        name=body.func.__name__ if isinstance(body, functools.partial) else body.__name__,
    )(*operands)


def dot(first, second, contract, precision=None):
    return lax.dot_general(
        first, second, (contract, ((), ())), precision=precision, preferred_element_type=F32
    )


def eye():
    return (
        lax.broadcasted_iota(jnp.int32, (LANES, LANES), 0)
        == lax.broadcasted_iota(jnp.int32, (LANES, LANES), 1)
    )


def to_column(row):
    column = jnp.sum(jnp.where(eye(), jnp.broadcast_to(row, (LANES, LANES)), 0.0), axis=1, keepdims=True)
    return jnp.broadcast_to(column, (LANES, LANES))


def to_row(block):
    return jnp.sum(jnp.where(eye(), block, 0.0), axis=0, keepdims=True)


def gather_rows(order, start, count, pairs):
    @pl.loop(0, count // GATHER)
    def _(step):
        base = pl.multiple_of(step * GATHER, GATHER)
        picks = [order[0, start + base + k] for k in range(GATHER)]
        for source, target in pairs:
            target[pl.ds(base, GATHER), :] = jnp.concatenate(
                [source[pl.ds(pick, 1), :] for pick in picks], axis=0
            )


def scatter_rows(order, start, count, pairs):
    @pl.loop(0, count // GATHER)
    def _(step):
        base = pl.multiple_of(step * GATHER, GATHER)
        picks = [order[0, start + base + k] for k in range(GATHER)]
        for source, target in pairs:
            rows = source[pl.ds(base, GATHER), :]
            for k, pick in enumerate(picks):
                target[pl.ds(pick, 1), :] = rows[k : k + 1]


def chunked(rows, work):
    for start in range(0, rows, CHUNK):
        work(pl.ds(start, CHUNK))


def spread_stiff(stiff, target):
    for start in range(0, target.shape[0], LANES):
        target[pl.ds(start, LANES), :] = to_column(stiff[:, pl.ds(start, LANES)])


def split(value):
    top = value.astype(BF)
    return top, (value - top.astype(F32)).astype(BF)


def membership_table(members, levels):
    rows = lax.broadcasted_iota(jnp.int32, (levels, members.shape[1]), 0)
    return (rows == members[...]).astype(F32)


def split_partial(weighted, basis, wide):
    wide[:, :LANES], wide[:, LANES:] = split(weighted)
    both = dot(wide[...], basis[...], ((0,), (0,)))
    return both[:LANES] + both[LANES:]


def pack(value, dots):
    return jnp.concatenate([value[:, k : k + LANES] for k in range(0, value.shape[1], LANES)] + [dots], axis=0)


def unpack(rows, share):
    parts = [rows[k : k + share] for k in range(0, rows.shape[0] - 8, share)]
    return jnp.concatenate(parts, axis=1), rows[rows.shape[0] - 8 :]


def open_faces(order_far, rhs_far, stiff_far, *rest):
    blocks, (order, rhs, stiff, own_stiff, face_stiff, sems) = rest[:4], rest[4:]
    fetches = [
        pltpu.make_async_copy(source, target, sems.at[k])
        for k, (source, target) in enumerate(((order_far, order), (rhs_far, rhs), (stiff_far, stiff)))
    ]
    for fetch in fetches:
        fetch.start()
    face = rhs.shape[0] // 4
    fetches[2].wait()
    spread_stiff(stiff, own_stiff)
    fetches[0].wait()
    fetches[1].wait()
    for k, block in enumerate(blocks):
        gather_rows(order, k * face, face, [(rhs, block), (own_stiff, face_stiff)])
        block[pl.ds(face, block.shape[0] - face), :] = jnp.concatenate(
            [to_row(face_stiff[pl.ds(t, LANES), :]) for t in range(0, face, LANES)]
            + [jnp.zeros((block.shape[0] - face - face // LANES, LANES), F32)],
            axis=0,
        )


def open_place(order, start, blocks, face, residual, other, face_stiff):
    for k, block in enumerate(blocks):
        for t in range(face // LANES):
            face_stiff[pl.ds(t * LANES, LANES), :] = to_column(block[pl.ds(face + t, 1), :])
        scatter_rows(order, start + k * face, face, [(block, residual), (face_stiff, other)])


def open_sub(order, one, two, residual, other, face_stiff):
    open_place(order, 0, (one, two), face_stiff.shape[0], residual, other, face_stiff)


def open_join(
    order, rhs, stiff, three, four, basis, placed, placed_stiff, residual, other, weight, weighted, partial, face_stiff, wide
):
    face = face_stiff.shape[0]
    open_place(order, 2 * face, (three, four), face, residual, other, face_stiff)
    spread_stiff(stiff, weight)
    residual[...] = rhs[...] + residual[...]
    weight[...] = weight[...] / (weight[...] + other[...])
    weighted[...] = weight[...] * residual[...]
    partial[...] = split_partial(weighted[...], basis, wide)


def sweeps(matrix, weighted, diagonal, fix, wide):
    fix[...] = weighted[...] / diagonal[...]
    for _ in range(LOCAL_STEPS):
        wide[:, :LANES], wide[:, LANES:] = split(fix[...])

        def work(rows):
            both = dot(matrix[rows, :], wide[...], ((1,), (0,)))
            product = both[:, :LANES] + both[:, LANES:]
            fix[rows, :] = fix[rows, :] + (weighted[rows, :] - product) / diagonal[rows, :]

        chunked(matrix.shape[0], work)


def prepare(matrix, members, inverse_two, rhs, diagonal, table_two, kept):
    kept[...] = rhs[...]
    table = membership_table(members, inverse_two.shape[0])
    table_two[...] = dot(inverse_two[...], table, ((0,), (0,)), HIGH)
    for start in range(0, matrix.shape[0], LANES):
        square = matrix[pl.ds(start, LANES), pl.ds(start, LANES)].astype(F32)
        column = jnp.sum(jnp.where(eye(), square, 0.0), axis=1, keepdims=True)
        diagonal[pl.ds(start, LANES), :] = jnp.broadcast_to(column, (LANES, LANES))


def local_fix(matrix, weighted, diagonal, total, inverse_one, fix, part_one, wide):
    part_one[...] = dot(total[...], inverse_one[...], ((1,), (1,)), HIGH)
    sweeps(matrix, weighted, diagonal, fix, wide)


def add_coarse(basis, coarse, weight, fix, local):
    narrow = coarse.astype(BF)

    def work(rows):
        correction = dot(basis[rows, :], narrow, ((1,), (1,)))
        local[rows, :] = weight[rows, :] * (fix[rows, :] + correction)

    chunked(basis.shape[0], work)


def send_grp(order, source, blocks):
    face = source.shape[0] // 4
    for k, block in enumerate(blocks):
        gather_rows(order, (2 + k) * face, face, [(source, block)])


def send_sub(order, source, *blocks):
    face = source.shape[0] // 4
    for k, block in enumerate(blocks):
        gather_rows(order, k * face, face, [(source, block)])


def place_sub(order, blocks, target):
    face = blocks[0].shape[0]
    for k, block in enumerate(blocks):
        scatter_rows(order, k * face, face, [(block, target)])


def place_grp(order, three, four, target):
    face = three.shape[0]
    for k, block in enumerate((three, four)):
        scatter_rows(order, (2 + k) * face, face, [(block, target)])


def first_local(order, weight, fix, basis, coarse, local, *blocks):
    add_coarse(basis, coarse[...], weight, fix, local)
    send_grp(order, local, blocks)


def apply_schur(matrix, vector, product, wide):
    wide[:, :LANES], wide[:, LANES:] = split(vector[...])

    def work(rows):
        both = dot(matrix[rows, :], wide[...], ((1,), (0,)))
        product[rows, :] = both[:, :LANES] + both[:, LANES:]

    chunked(matrix.shape[0], work)


def column_sum(first, second):
    return jnp.sum(first[...] * second[...], axis=0, keepdims=True)


def first_apply(order, matrix, local, residual, one, two, placed, z_value, product, dots, *rest):
    blocks, wide = rest[:2], rest[2]
    place_sub(order, (one, two), z_value)
    z_value[...] = local[...] + z_value[...]
    apply_schur(matrix, z_value, product, wide)
    send_grp(order, product, blocks)
    dots[...] = jnp.concatenate(
        [0.5 * column_sum(residual, z_value), column_sum(z_value, product), jnp.zeros((6, LANES), F32)], axis=0
    )


def image_partial(order, product, weight, one, two, placed, basis, dots, image, weighted, payload, wide):
    place_sub(order, (one, two), image)
    image[...] = product[...] + image[...]
    weighted[...] = weight[...] * image[...]
    value = split_partial(weighted[...], basis, wide)
    share = value.shape[0] // payload.shape[0]
    for k in range(payload.shape[0]):
        payload[k] = pack(value[k * share : (k + 1) * share], dots[...])


def first_groups(chunks, members, total, part, *, levels):
    total[...] = jnp.sum(chunks[...], axis=0)
    part[...] = dot(total[...], membership_table(members, levels), ((1,), (1,)), HIGH)


def second_groups(chunks, members, total, part, *, levels):
    total[...], dots = unpack(jnp.sum(chunks[...], axis=0), total.shape[0])
    part[...] = pack(dot(total[...], membership_table(members, levels), ((1,), (1,)), HIGH), dots)


def copy_row(*refs):
    *parts, copies = refs
    dots = parts[0][...]
    for other in parts[1:]:
        dots = dots + other[...]
    row = jnp.concatenate([dots[k : k + 1] for k in range(3)], axis=1)
    for k in range(copies.shape[0]):
        copies[k] = row


def add_and_copy(*refs):
    value = refs[0][...]
    for other in refs[1:-1]:
        value = value + other[...]
    for k in range(refs[-1].shape[0]):
        refs[-1][k] = value


def first_coarse(chunks, part_one, table_two, value, copies):
    value[...] = part_one[...] + dot(jnp.sum(chunks[...], axis=0), table_two[...], ((1,), (0,)), HIGH)
    for k in range(copies.shape[0]):
        copies[k] = value[...]


def second_coarse(chunks, part_one, value, table_two, copies, info, column):
    share = value.shape[0]
    two, dots = unpack(jnp.sum(chunks[...], axis=0), share)
    step = dots[0:1] / dots[1:2]
    info[...] = jnp.concatenate([dots[0:2], step, dots[3:]], axis=0)
    column[...] = to_column(step)
    mine = column[pl.ds(pl.multiple_of(lax.axis_index("sub") * share, 8), share), :][:, 0:1]
    solved = value[...] - mine * (part_one[...] + dot(two, table_two[...], ((1,), (0,)), HIGH))
    for k in range(copies.shape[0]):
        copies[k] = solved


def second_local(order, weight, basis, residual, image, fix_first, fix_image, coarse, info, residual_out, local, *rest):
    blocks, fix = rest[:2], rest[2]
    step = info[2:3]
    fix[...] = fix_first[...] - step * fix_image[...]
    add_coarse(basis, coarse[...], weight, fix, local)
    residual_out[...] = residual[...] - step * image[...]
    send_grp(order, local, blocks)


def second_apply(order, matrix, local, residual, z_first, one, two, placed, z_value, product, dots, *rest):
    blocks, wide = rest[:2], rest[2]
    place_sub(order, (one, two), z_value)
    z_value[...] = local[...] + z_value[...]
    apply_schur(matrix, z_value, product, wide)
    send_grp(order, product, blocks)
    dots[...] = jnp.concatenate(
        [
            0.5 * column_sum(residual, z_value),
            column_sum(z_value, product),
            column_sum(z_first, product),
            jnp.zeros((5, LANES), F32),
        ],
        axis=0,
    )


def last_image(order, product, one, two, placed, image):
    place_sub(order, (one, two), image)
    image[...] = product[...] + image[...]


def finish(chunks, info, z_first, z_second, image_first, image_second, residual, solution_out, residual_out):
    dots = jnp.sum(chunks[...], axis=0)
    rz_first, step_first = info[0:1], info[2:3]
    rz, zaz, zaz_first = (dots[:, k * LANES : (k + 1) * LANES] for k in range(3))
    ratio = rz / rz_first
    step = rz / (zaz + 2.0 * ratio * zaz_first + ratio * ratio * info[1:2])
    solution_out[...] = step_first * z_first[...] + step * (z_second[...] + ratio * z_first[...])
    residual_out[...] = residual[...] - step * (image_second[...] + ratio * image_first[...])


def passed_along(value, axis, steps):
    count = lax.axis_size(axis)
    pairs = [(source, (source + steps) % count) for source in range(count)]
    return lax.ppermute(value, axis, pairs)


def turned(value, step, inner):
    pairs = [(k, k // inner * inner + (k + step) % inner) for k in range(lax.axis_size("grp"))]
    return lax.ppermute(value, "grp", pairs)


def exchanged(blocks):
    return [
        passed_along(blocks[1], "sub", 1),
        passed_along(blocks[0], "sub", -1),
        passed_along(blocks[3], "grp", 1),
        passed_along(blocks[2], "grp", -1),
    ]


def spread(chunks, axis, groups=None):
    return lax.all_to_all(chunks, axis, 0, 0, axis_index_groups=groups)


def body(rhs, schur, stiff, face_index, basis, membership, level1_inv, level2_inv):
    matrix, rhs, basis = schur[0, 0], rhs[0, 0], basis[0, 0]
    order, stiff, members, inverse_one = face_index[0], stiff[0], membership, level1_inv[0]
    dofs, cols = rhs.shape
    face = dofs // 4
    coarse, levels = inverse_one.shape[0], level2_inv.shape[0]
    n_sub, n_grp = lax.axis_size("sub"), lax.axis_size("grp")
    inner = 4
    outer = n_grp // inner
    groups_z = [[z * inner + y for z in range(outer)] for y in range(inner)]
    share = cols // n_sub
    vector, block = shape(dofs, cols), shape(face, cols)
    face_rows = face + -(-face // LANES // 8) * 8
    product_flops = 2 * dofs * dofs * 2 * cols
    wide = pltpu.VMEM((dofs, 2 * cols), BF)

    def swap(source, toward_grp):
        three = passed_along(toward_grp[1], "grp", 1)
        four = passed_along(toward_grp[0], "grp", -1)
        first, second = kernel(send_sub, (order, source), [block] * 2)
        one = passed_along(second, "sub", 1)
        two = passed_along(first, "sub", -1)
        (placed,) = kernel(place_grp, (order, three, four), [vector])
        return one, two, placed

    blocks = kernel(
        open_faces,
        (order, rhs, stiff),
        [shape(face_rows, cols)] * 4,
        [
            pltpu.SMEM((1, dofs), jnp.int32),
            pltpu.VMEM((dofs, cols), F32),
            pltpu.VMEM((1, dofs), F32),
            pltpu.VMEM((dofs, cols), F32),
            pltpu.VMEM((face, cols), F32),
            pltpu.SemaphoreType.DMA((3,)),
        ],
        specs=[HB] * 3,
        limit=60,
    )
    first, matrix = lax.optimization_barrier((blocks[0], matrix))
    diagonal, table_two, kept = kernel(
        prepare, (matrix, members, level2_inv, rhs), [vector, shape(levels, coarse), vector], scalars=0
    )
    one, two, three, four = exchanged([first, *blocks[1:]])
    placed = kernel(open_sub, (order, one, two), [vector, vector], [pltpu.VMEM((face, cols), F32)])
    three, four, diagonal, table_two, kept = lax.optimization_barrier((three, four, diagonal, table_two, kept))
    residual0, _, weight, weighted, partial = kernel(
        open_join,
        (order, kept, stiff, three, four, basis, *placed),
        [vector] * 4 + [shape(cols, coarse)],
        [pltpu.VMEM((face, cols), F32), wide],
        aliases={6: 0, 7: 1},
    )

    def to_groups(body, chunks, weighted):
        chunks = spread(chunks, "sub")
        part_shape = chunks.shape[1:] if chunks.shape[2] == LANES else (share, levels)
        total, part = kernel(
            functools.partial(body, levels=levels),
            (chunks, members),
            [shape(share, coarse), shape(*part_shape)],
            scalars=0,
        )
        part, total, weighted = lax.optimization_barrier((part, total, weighted))
        others = [turned(part, step, inner) for step in range(1, inner)]
        fix, part_one = kernel(
            local_fix,
            (matrix, weighted, diagonal, total, inverse_one),
            [vector, shape(share, coarse)],
            [wide],
            scalars=0,
            flops=2 * product_flops,
        )
        *others, fix = lax.optimization_barrier((*others, fix))
        (copies,) = kernel(add_and_copy, (part, *others), [shape(outer, *part_shape)], scalars=0)
        return part_one, spread(copies, "grp", groups_z), fix

    def from_groups(copies):
        return spread(copies, "sub").reshape(cols, copies.shape[2])

    part_one, chunks, fix0 = to_groups(first_groups, partial.reshape(n_sub, share, coarse), weighted)
    value0, copies = kernel(
        first_coarse,
        (chunks, part_one, table_two),
        [shape(share, coarse), shape(n_sub, share, coarse)],
        scalars=0,
    )
    coarse0 = from_groups(copies)
    local, *blocks = kernel(first_local, (order, weight, fix0, basis, coarse0), [vector] + [block] * 2)

    z0, product0, dots, *blocks = kernel(
        first_apply,
        (order, matrix, local, residual0, *swap(local, blocks)),
        [vector, vector, shape(8, cols)] + [block] * 2,
        [wide],
        flops=product_flops,
        aliases={6: 0},
    )
    image0, weighted, payload = kernel(
        image_partial,
        (order, product0, weight, *swap(product0, blocks), basis, dots),
        [vector, vector, shape(n_sub, share * coarse // LANES + 8, LANES)],
        [wide],
        aliases={5: 0},
    )
    part_one, chunks, fix_image = to_groups(second_groups, payload, weighted)
    copies, info = kernel(
        second_coarse,
        (chunks, part_one, value0, table_two),
        [shape(n_sub, share, coarse), shape(8, cols)],
        [pltpu.VMEM((LANES, LANES), F32)],
        scalars=0,
    )
    coarse1 = from_groups(copies)
    residual1, local, *blocks = kernel(
        second_local,
        (order, weight, basis, residual0, image0, fix0, fix_image, coarse1, info),
        [vector, vector] + [block] * 2,
        [pltpu.VMEM((dofs, cols), F32)],
    )
    z1, product1, dots, *blocks = kernel(
        second_apply,
        (order, matrix, local, residual1, z0, *swap(local, blocks)),
        [vector, vector, shape(8, cols)] + [block] * 2,
        [wide],
        flops=product_flops,
        aliases={7: 0},
    )
    dots = dots + lax.ppermute(dots, "sub", [(k, k ^ 1) for k in range(n_sub)])
    blocks[0], dots = lax.optimization_barrier((blocks[0], dots))
    dots = [dots] + [passed_along(dots, "sub", step) for step in range(2, n_sub, 2)]
    arrived = swap(product1, blocks)
    (image1,) = kernel(last_image, (order, product1, *arrived), [vector], aliases={4: 0})
    *dots, image1 = lax.optimization_barrier((*dots, image1))
    (copies,) = kernel(copy_row, dots, [shape(n_grp, 1, 3 * cols)], scalars=0)
    chunks = spread(copies, "grp")
    outs = kernel(
        finish, (chunks, info, z0, z1, image0, image1, residual1), [vector, vector], scalars=0
    )
    return outs[0][None, None], outs[1][None, None]


def solution(mesh):
    placed = (
        P("grp", "sub", None, None),
        P("grp", "sub", None, None),
        P("grp", "sub", None),
        P("grp", "sub", None),
        P("grp", "sub", None, None),
        P("grp", None),
        P("grp", None, None),
        P(),
    )
    return jax.shard_map(
        body,
        mesh=mesh,
        in_specs=placed,
        out_specs=(P("grp", "sub", None, None), P("grp", "sub", None, None)),
        check_vma=False,
    )
```

```python
import functools

import jax
import jax.numpy as jnp
from jax import lax
from jax.experimental import pallas as pl
from jax.experimental.pallas import tpu as pltpu
from jax.sharding import PartitionSpec as P

LOCAL_STEPS = 2
HIGH = lax.Precision.HIGHEST
BF = jnp.bfloat16
F32 = jnp.float32
LANES = 128
GATHER = 64
CHUNK = 256
VM = pl.BlockSpec(memory_space=pltpu.VMEM)
SM = pl.BlockSpec(memory_space=pltpu.SMEM)
HB = pl.BlockSpec(memory_space=pltpu.HBM)


def shape(*dims, kind=F32):
    return jax.ShapeDtypeStruct(dims, kind)


def kernel(body, operands, outs, scratch=(), limit=10, scalars=1, flops=0, aliases=None, specs=None):
    specs = specs or [SM] * scalars + [VM] * (len(operands) - scalars)
    moved = sum(value.size * value.dtype.itemsize for value in (*operands, *outs))
    return pl.pallas_call(
        body,
        out_shape=list(outs),
        in_specs=specs,
        out_specs=[VM] * len(outs),
        scratch_shapes=list(scratch),
        input_output_aliases=aliases or {},
        compiler_params=pltpu.CompilerParams(vmem_limit_bytes=limit << 20),
        cost_estimate=pl.CostEstimate(flops=flops, bytes_accessed=moved, transcendentals=0),
        name=body.func.__name__ if isinstance(body, functools.partial) else body.__name__,
    )(*operands)


def dot(first, second, contract, precision=None):
    return lax.dot_general(
        first, second, (contract, ((), ())), precision=precision, preferred_element_type=F32
    )


def eye():
    return (
        lax.broadcasted_iota(jnp.int32, (LANES, LANES), 0)
        == lax.broadcasted_iota(jnp.int32, (LANES, LANES), 1)
    )


def to_column(row):
    column = jnp.sum(jnp.where(eye(), jnp.broadcast_to(row, (LANES, LANES)), 0.0), axis=1, keepdims=True)
    return jnp.broadcast_to(column, (LANES, LANES))


def to_row(block):
    return jnp.sum(jnp.where(eye(), block, 0.0), axis=0, keepdims=True)


def gather_rows(order, start, count, pairs):
    @pl.loop(0, count // GATHER)
    def _(step):
        base = pl.multiple_of(step * GATHER, GATHER)
        picks = [order[0, start + base + k] for k in range(GATHER)]
        for source, target in pairs:
            target[pl.ds(base, GATHER), :] = jnp.concatenate(
                [source[pl.ds(pick, 1), :] for pick in picks], axis=0
            )


def scatter_rows(order, start, count, pairs):
    @pl.loop(0, count // GATHER)
    def _(step):
        base = pl.multiple_of(step * GATHER, GATHER)
        picks = [order[0, start + base + k] for k in range(GATHER)]
        for source, target in pairs:
            rows = source[pl.ds(base, GATHER), :]
            for k, pick in enumerate(picks):
                target[pl.ds(pick, 1), :] = rows[k : k + 1]


def chunked(rows, work):
    for start in range(0, rows, CHUNK):
        work(pl.ds(start, CHUNK))


def spread_stiff(stiff, target):
    for start in range(0, target.shape[0], LANES):
        target[pl.ds(start, LANES), :] = to_column(stiff[:, pl.ds(start, LANES)])


def split(value):
    top = value.astype(BF)
    return top, (value - top.astype(F32)).astype(BF)


def membership_table(members, levels):
    rows = lax.broadcasted_iota(jnp.int32, (levels, members.shape[1]), 0)
    return (rows == members[...]).astype(F32)


def split_partial(weighted, basis, wide):
    wide[:, :LANES], wide[:, LANES:] = split(weighted)
    both = dot(wide[...], basis[...], ((0,), (0,)))
    return both[:LANES] + both[LANES:]


def pack(value, dots):
    return jnp.concatenate([value[:, k : k + LANES] for k in range(0, value.shape[1], LANES)] + [dots], axis=0)


def unpack(rows, share):
    parts = [rows[k : k + share] for k in range(0, rows.shape[0] - 8, share)]
    return jnp.concatenate(parts, axis=1), rows[rows.shape[0] - 8 :]


def open_faces(order_far, rhs_far, stiff_far, *rest):
    blocks, (order, rhs, stiff, own_stiff, face_stiff, sems) = rest[:4], rest[4:]
    fetches = [
        pltpu.make_async_copy(source, target, sems.at[k])
        for k, (source, target) in enumerate(((order_far, order), (rhs_far, rhs), (stiff_far, stiff)))
    ]
    for fetch in fetches:
        fetch.start()
    face = rhs.shape[0] // 4
    fetches[2].wait()
    spread_stiff(stiff, own_stiff)
    fetches[0].wait()
    fetches[1].wait()
    for k, block in enumerate(blocks):
        gather_rows(order, k * face, face, [(rhs, block), (own_stiff, face_stiff)])
        block[pl.ds(face, block.shape[0] - face), :] = jnp.concatenate(
            [to_row(face_stiff[pl.ds(t, LANES), :]) for t in range(0, face, LANES)]
            + [jnp.zeros((block.shape[0] - face - face // LANES, LANES), F32)],
            axis=0,
        )


def open_place(order, start, blocks, face, residual, other, face_stiff):
    for k, block in enumerate(blocks):
        for t in range(face // LANES):
            face_stiff[pl.ds(t * LANES, LANES), :] = to_column(block[pl.ds(face + t, 1), :])
        scatter_rows(order, start + k * face, face, [(block, residual), (face_stiff, other)])


def open_sub(order, one, two, residual, other, face_stiff):
    open_place(order, 0, (one, two), face_stiff.shape[0], residual, other, face_stiff)


def open_join(
    order, rhs, stiff, three, four, basis, placed, placed_stiff, residual, other, weight, weighted, partial, face_stiff, wide
):
    face = face_stiff.shape[0]
    open_place(order, 2 * face, (three, four), face, residual, other, face_stiff)
    spread_stiff(stiff, weight)
    residual[...] = rhs[...] + residual[...]
    weight[...] = weight[...] / (weight[...] + other[...])
    weighted[...] = weight[...] * residual[...]
    partial[...] = split_partial(weighted[...], basis, wide)


def sweeps(matrix, weighted, diagonal, fix, wide):
    fix[...] = weighted[...] / diagonal[...]
    for _ in range(LOCAL_STEPS):
        wide[:, :LANES], wide[:, LANES:] = split(fix[...])

        def work(rows):
            both = dot(matrix[rows, :], wide[...], ((1,), (0,)))
            product = both[:, :LANES] + both[:, LANES:]
            fix[rows, :] = fix[rows, :] + (weighted[rows, :] - product) / diagonal[rows, :]

        chunked(matrix.shape[0], work)


def prepare(matrix, members, inverse_two, rhs, diagonal, table_two, kept):
    kept[...] = rhs[...]
    table = membership_table(members, inverse_two.shape[0])
    table_two[...] = dot(inverse_two[...], table, ((0,), (0,)), HIGH)
    for start in range(0, matrix.shape[0], LANES):
        square = matrix[pl.ds(start, LANES), pl.ds(start, LANES)].astype(F32)
        column = jnp.sum(jnp.where(eye(), square, 0.0), axis=1, keepdims=True)
        diagonal[pl.ds(start, LANES), :] = jnp.broadcast_to(column, (LANES, LANES))


def local_fix(matrix, weighted, diagonal, total, inverse_one, fix, part_one, wide):
    part_one[...] = dot(total[...], inverse_one[...], ((1,), (1,)), HIGH)
    sweeps(matrix, weighted, diagonal, fix, wide)


def add_coarse(basis, coarse, weight, fix, local):
    narrow = coarse.astype(BF)

    def work(rows):
        correction = dot(basis[rows, :], narrow, ((1,), (1,)))
        local[rows, :] = weight[rows, :] * (fix[rows, :] + correction)

    chunked(basis.shape[0], work)


def send_grp(order, source, blocks):
    face = source.shape[0] // 4
    for k, block in enumerate(blocks):
        gather_rows(order, (2 + k) * face, face, [(source, block)])


def send_sub(order, source, *blocks):
    face = source.shape[0] // 4
    for k, block in enumerate(blocks):
        gather_rows(order, k * face, face, [(source, block)])


def place_sub(order, blocks, target):
    face = blocks[0].shape[0]
    for k, block in enumerate(blocks):
        scatter_rows(order, k * face, face, [(block, target)])


def place_grp(order, three, four, target):
    face = three.shape[0]
    for k, block in enumerate((three, four)):
        scatter_rows(order, (2 + k) * face, face, [(block, target)])


def first_local(order, weight, fix, basis, coarse, local, *blocks):
    add_coarse(basis, coarse[...], weight, fix, local)
    send_grp(order, local, blocks)


def apply_schur(matrix, vector, product, wide):
    wide[:, :LANES], wide[:, LANES:] = split(vector[...])

    def work(rows):
        both = dot(matrix[rows, :], wide[...], ((1,), (0,)))
        product[rows, :] = both[:, :LANES] + both[:, LANES:]

    chunked(matrix.shape[0], work)


def column_sum(first, second):
    return jnp.sum(first[...] * second[...], axis=0, keepdims=True)


def first_apply(order, matrix, local, residual, one, two, placed, z_value, product, dots, *rest):
    blocks, wide = rest[:2], rest[2]
    place_sub(order, (one, two), z_value)
    z_value[...] = local[...] + z_value[...]
    apply_schur(matrix, z_value, product, wide)
    send_grp(order, product, blocks)
    dots[...] = jnp.concatenate(
        [0.5 * column_sum(residual, z_value), column_sum(z_value, product), jnp.zeros((6, LANES), F32)], axis=0
    )


def image_partial(order, product, weight, one, two, placed, basis, dots, image, weighted, payload, wide):
    place_sub(order, (one, two), image)
    image[...] = product[...] + image[...]
    weighted[...] = weight[...] * image[...]
    value = split_partial(weighted[...], basis, wide)
    share = value.shape[0] // payload.shape[0]
    for k in range(payload.shape[0]):
        payload[k] = pack(value[k * share : (k + 1) * share], dots[...])


def first_groups(chunks, members, total, part, *, levels):
    total[...] = jnp.sum(chunks[...], axis=0)
    part[...] = dot(total[...], membership_table(members, levels), ((1,), (1,)), HIGH)


def second_groups(chunks, members, total, part, *, levels):
    total[...], dots = unpack(jnp.sum(chunks[...], axis=0), total.shape[0])
    part[...] = pack(dot(total[...], membership_table(members, levels), ((1,), (1,)), HIGH), dots)


def copy_row(*refs):
    *parts, copies = refs
    dots = parts[0][...]
    for other in parts[1:]:
        dots = dots + other[...]
    row = jnp.concatenate([dots[k : k + 1] for k in range(3)], axis=1)
    for k in range(copies.shape[0]):
        copies[k] = row


def add_and_copy(*refs):
    value = refs[0][...]
    for other in refs[1:-1]:
        value = value + other[...]
    for k in range(refs[-1].shape[0]):
        refs[-1][k] = value


def first_coarse(chunks, part_one, table_two, value, copies):
    value[...] = part_one[...] + dot(jnp.sum(chunks[...], axis=0), table_two[...], ((1,), (0,)), HIGH)
    for k in range(copies.shape[0]):
        copies[k] = value[...]


def second_coarse(chunks, part_one, value, table_two, copies, info, column):
    share = value.shape[0]
    two, dots = unpack(jnp.sum(chunks[...], axis=0), share)
    step = dots[0:1] / dots[1:2]
    info[...] = jnp.concatenate([dots[0:2], step, dots[3:]], axis=0)
    column[...] = to_column(step)
    mine = column[pl.ds(pl.multiple_of(lax.axis_index("sub") * share, 8), share), :][:, 0:1]
    solved = value[...] - mine * (part_one[...] + dot(two, table_two[...], ((1,), (0,)), HIGH))
    for k in range(copies.shape[0]):
        copies[k] = solved


def second_local(order, weight, basis, residual, image, fix_first, fix_image, coarse, info, residual_out, local, *rest):
    blocks, fix = rest[:2], rest[2]
    step = info[2:3]
    fix[...] = fix_first[...] - step * fix_image[...]
    add_coarse(basis, coarse[...], weight, fix, local)
    residual_out[...] = residual[...] - step * image[...]
    send_grp(order, local, blocks)


def second_apply(order, matrix, local, residual, z_first, one, two, placed, z_value, product, dots, *rest):
    blocks, wide = rest[:2], rest[2]
    place_sub(order, (one, two), z_value)
    z_value[...] = local[...] + z_value[...]
    apply_schur(matrix, z_value, product, wide)
    send_grp(order, product, blocks)
    dots[...] = jnp.concatenate(
        [
            0.5 * column_sum(residual, z_value),
            column_sum(z_value, product),
            column_sum(z_first, product),
            jnp.zeros((5, LANES), F32),
        ],
        axis=0,
    )


def last_image(order, product, one, two, placed, image):
    place_sub(order, (one, two), image)
    image[...] = product[...] + image[...]


def finish(chunks, info, z_first, z_second, image_first, image_second, residual, solution_out, residual_out):
    dots = jnp.sum(chunks[...], axis=0)
    rz_first, step_first = info[0:1], info[2:3]
    rz, zaz, zaz_first = (dots[:, k * LANES : (k + 1) * LANES] for k in range(3))
    ratio = rz / rz_first
    step = rz / (zaz + 2.0 * ratio * zaz_first + ratio * ratio * info[1:2])
    solution_out[...] = step_first * z_first[...] + step * (z_second[...] + ratio * z_first[...])
    residual_out[...] = residual[...] - step * (image_second[...] + ratio * image_first[...])


def passed_along(value, axis, steps):
    count = lax.axis_size(axis)
    pairs = [(source, (source + steps) % count) for source in range(count)]
    return lax.ppermute(value, axis, pairs)


def turned(value, step, inner):
    pairs = [(k, k // inner * inner + (k + step) % inner) for k in range(lax.axis_size("grp"))]
    return lax.ppermute(value, "grp", pairs)


def exchanged(blocks):
    return [
        passed_along(blocks[1], "sub", 1),
        passed_along(blocks[0], "sub", -1),
        passed_along(blocks[3], "grp", 1),
        passed_along(blocks[2], "grp", -1),
    ]


def spread(chunks, axis, groups=None):
    return lax.all_to_all(chunks, axis, 0, 0, axis_index_groups=groups)


def body(rhs, schur, stiff, face_index, basis, membership, level1_inv, level2_inv):
    matrix, rhs, basis = schur[0, 0], rhs[0, 0], basis[0, 0]
    order, stiff, members, inverse_one = face_index[0], stiff[0], membership, level1_inv[0]
    dofs, cols = rhs.shape
    face = dofs // 4
    coarse, levels = inverse_one.shape[0], level2_inv.shape[0]
    n_sub, n_grp = lax.axis_size("sub"), lax.axis_size("grp")
    inner = 4
    outer = n_grp // inner
    groups_z = [[z * inner + y for z in range(outer)] for y in range(inner)]
    share = cols // n_sub
    vector, block = shape(dofs, cols), shape(face, cols)
    face_rows = face + -(-face // LANES // 8) * 8
    product_flops = 2 * dofs * dofs * 2 * cols
    wide = pltpu.VMEM((dofs, 2 * cols), BF)

    def swap(source, toward_grp):
        three = passed_along(toward_grp[1], "grp", 1)
        four = passed_along(toward_grp[0], "grp", -1)
        first, second = kernel(send_sub, (order, source), [block] * 2)
        one = passed_along(second, "sub", 1)
        two = passed_along(first, "sub", -1)
        (placed,) = kernel(place_grp, (order, three, four), [vector])
        return one, two, placed

    blocks = kernel(
        open_faces,
        (order, rhs, stiff),
        [shape(face_rows, cols)] * 4,
        [
            pltpu.SMEM((1, dofs), jnp.int32),
            pltpu.VMEM((dofs, cols), F32),
            pltpu.VMEM((1, dofs), F32),
            pltpu.VMEM((dofs, cols), F32),
            pltpu.VMEM((face, cols), F32),
            pltpu.SemaphoreType.DMA((3,)),
        ],
        specs=[HB] * 3,
        limit=60,
    )
    first, matrix = lax.optimization_barrier((blocks[0], matrix))
    diagonal, table_two, kept = kernel(
        prepare, (matrix, members, level2_inv, rhs), [vector, shape(levels, coarse), vector], scalars=0
    )
    one, two, three, four = exchanged([first, *blocks[1:]])
    placed = kernel(open_sub, (order, one, two), [vector, vector], [pltpu.VMEM((face, cols), F32)])
    three, four, diagonal, table_two, kept = lax.optimization_barrier((three, four, diagonal, table_two, kept))
    residual0, _, weight, weighted, partial = kernel(
        open_join,
        (order, kept, stiff, three, four, basis, *placed),
        [vector] * 4 + [shape(cols, coarse)],
        [pltpu.VMEM((face, cols), F32), wide],
        aliases={6: 0, 7: 1},
    )

    def to_groups(body, chunks, weighted):
        chunks = spread(chunks, "sub")
        part_shape = chunks.shape[1:] if chunks.shape[2] == LANES else (share, levels)
        total, part = kernel(
            functools.partial(body, levels=levels),
            (chunks, members),
            [shape(share, coarse), shape(*part_shape)],
            scalars=0,
        )
        part, total, weighted = lax.optimization_barrier((part, total, weighted))
        others = [turned(part, step, inner) for step in range(1, inner)]
        fix, part_one = kernel(
            local_fix,
            (matrix, weighted, diagonal, total, inverse_one),
            [vector, shape(share, coarse)],
            [wide],
            scalars=0,
            flops=2 * product_flops,
        )
        *others, fix = lax.optimization_barrier((*others, fix))
        (copies,) = kernel(add_and_copy, (part, *others), [shape(outer, *part_shape)], scalars=0)
        return part_one, spread(copies, "grp", groups_z), fix

    def from_groups(copies):
        return spread(copies, "sub").reshape(cols, copies.shape[2])

    part_one, chunks, fix0 = to_groups(first_groups, partial.reshape(n_sub, share, coarse), weighted)
    value0, copies = kernel(
        first_coarse,
        (chunks, part_one, table_two),
        [shape(share, coarse), shape(n_sub, share, coarse)],
        scalars=0,
    )
    coarse0 = from_groups(copies)
    local, *blocks = kernel(first_local, (order, weight, fix0, basis, coarse0), [vector] + [block] * 2)

    z0, product0, dots, *blocks = kernel(
        first_apply,
        (order, matrix, local, residual0, *swap(local, blocks)),
        [vector, vector, shape(8, cols)] + [block] * 2,
        [wide],
        flops=product_flops,
        aliases={6: 0},
    )
    image0, weighted, payload = kernel(
        image_partial,
        (order, product0, weight, *swap(product0, blocks), basis, dots),
        [vector, vector, shape(n_sub, share * coarse // LANES + 8, LANES)],
        [wide],
        aliases={5: 0},
    )
    part_one, chunks, fix_image = to_groups(second_groups, payload, weighted)
    copies, info = kernel(
        second_coarse,
        (chunks, part_one, value0, table_two),
        [shape(n_sub, share, coarse), shape(8, cols)],
        [pltpu.VMEM((LANES, LANES), F32)],
        scalars=0,
    )
    coarse1 = from_groups(copies)
    residual1, local, *blocks = kernel(
        second_local,
        (order, weight, basis, residual0, image0, fix0, fix_image, coarse1, info),
        [vector, vector] + [block] * 2,
        [pltpu.VMEM((dofs, cols), F32)],
    )
    z1, product1, dots, *blocks = kernel(
        second_apply,
        (order, matrix, local, residual1, z0, *swap(local, blocks)),
        [vector, vector, shape(8, cols)] + [block] * 2,
        [wide],
        flops=product_flops,
        aliases={7: 0},
    )
    dots = dots + lax.ppermute(dots, "sub", [(k, k ^ 1) for k in range(n_sub)])
    dots = [dots] + [passed_along(dots, "sub", step) for step in range(2, n_sub, 2)]
    arrived = swap(product1, blocks)
    (image1,) = kernel(last_image, (order, product1, *arrived), [vector], aliases={4: 0})
    *dots, image1 = lax.optimization_barrier((*dots, image1))
    (copies,) = kernel(copy_row, dots, [shape(n_grp, 1, 3 * cols)], scalars=0)
    chunks = spread(copies, "grp")
    outs = kernel(
        finish, (chunks, info, z0, z1, image0, image1, residual1), [vector, vector], scalars=0
    )
    return outs[0][None, None], outs[1][None, None]


def solution(mesh):
    placed = (
        P("grp", "sub", None, None),
        P("grp", "sub", None, None),
        P("grp", "sub", None),
        P("grp", "sub", None),
        P("grp", "sub", None, None),
        P("grp", None),
        P("grp", None, None),
        P(),
    )
    return jax.shard_map(
        body,
        mesh=mesh,
        in_specs=placed,
        out_specs=(P("grp", "sub", None, None), P("grp", "sub", None, None)),
        check_vma=False,
    )
```
